256 devices in a mesh: gx: 16 (over z, core), gy: 16 (over x, y).
Axes of the slice: x: 4, y: 4, z: 8, core: 2. Of those that a mesh axis runs over, the one named last changes fastest.
Arguments:
- tracers: bfloat16 [8, 128, 128, 256], P(None, 'gx', 'gy'), may hold values from -6 to 6
- velocity: float32 [2, 128, 128], P(None, 'gx', 'gy'), may hold values from -0.04 to 0.04
- inflow: int32 [4, 128, 128], P(None, 'gx', 'gy'), may hold values from 0 to 1, as said below
- leaf_solve: float32 [256, 256], replicated, may hold values from -0.375 to 0.375
- leaf_skeleton: float32 [256, 64], replicated, may hold values from -0.375 to 0.375
- leaf_lift: float32 [64, 256], replicated, may hold values from -0.75 to 0.75
- merge_first: float32 [128, 64], replicated, may hold values from -0.5 to 0.5
- merge_second: float32 [128, 128], replicated, may hold values from -0.5 to 0.5
- merge_rest: float32 [12, 256, 128], replicated, may hold values from -0.375 to 0.375
- parent_first: float32 [64, 128], replicated, may hold values from -0.75 to 0.75
- parent_second: float32 [128, 128], replicated, may hold values from -0.5 to 0.5
- parent_rest: float32 [12, 128, 256], replicated, may hold values from -0.5 to 0.5
- sibling_first: float32 [128, 128], replicated, may hold values from -0.125 to 0.125
- sibling_second: float32 [128, 128], replicated, may hold values from -0.125 to 0.125
- sibling_rest: float32 [12, 256, 256], replicated, may hold values from -0.09375 to 0.09375
- root_map: float32 [128, 128], replicated, may hold values from -0.5 to 0.5
Outputs:
- updated: bfloat16 [8, 128, 128, 256], P(None, 'gx', 'gy')
The draws below stay inside these ranges and needn't reach their ends.
Inputs may be any that keep to these rules, and one draw needn't show every extreme that they name: inflow[0] of leaf (i, j) equals 1 minus inflow[1] of leaf (i - 1, j), and inflow[2] of leaf (i, j) equals 1 minus inflow[3] of leaf (i, j - 1); inflow[1] is 0 on the last leaves along the first dimension and inflow[3] on the last leaves along the second.
All inputs are finite; a program needn't handle non-finite values.
Results may differ from the reference program's by a relative error of at most 0.001.
Values may be sent and summed in bfloat16 or wider, within the bound.
No kernel may reach another device: no remote copies, remote signals or barrier semaphores. Data moves between devices by JAX's collectives and lax.ppermute only.
A program may use at most 64 MiB of HBM per device.

```python
import jax
import jax.numpy as jnp
from jax import lax

TRACERS = 8
NODE = 16
NODES = 256
LEAF_SKEL = 64
RANK = 128
LEAF_SIDE = 8
LEAVES_X = 128
LEAVES_Y = 128
LEVELS = 14
N_GX = 16
N_GY = 16


def draw_inflow(key, part):
    key_first, key_second = jax.random.split(jax.random.fold_in(key, 11))
    low_first = jax.random.randint(key_first, (LEAVES_X, LEAVES_Y), 0, 2, dtype=jnp.int32)
    low_second = jax.random.randint(key_second, (LEAVES_X, LEAVES_Y), 0, 2, dtype=jnp.int32)
    high_first = jnp.concatenate([1 - low_first[1:], jnp.zeros((1, LEAVES_Y), jnp.int32)], axis=0)
    high_second = jnp.concatenate([1 - low_second[:, 1:], jnp.zeros((LEAVES_X, 1), jnp.int32)], axis=1)
    return jnp.stack([low_first, high_first, low_second, high_second]).astype(jnp.int32)


def shard_levels(key, extent, shards, least, top_value):
    level = 1.0
    for dim, blocks in shards:
        heights = jax.random.uniform(jax.random.fold_in(jax.random.fold_in(key, 6), dim), (blocks,), jnp.float32, least / len(shards), top_value / len(shards))
        level = level * jnp.repeat(jnp.exp(heights), extent[dim] // blocks).reshape((-1,) + (1,) * (len(extent) - 1 - dim))
    return level


def normal_values(stream_key, dims, deviation, most, cuts=(), held_as=jnp.bfloat16):
    result = jax.random.normal(stream_key, dims, jnp.float32) * deviation
    if len(cuts) > 0:
        result = shard_levels(stream_key, dims, cuts, -0.22, 0.18) * result
    return jnp.clip(result, min=-most, max=most).astype(held_as)


def setup_inputs(seed: int = 0) -> dict:
    seeds = jax.random.split(jax.random.key(seed), 17)
    return {
        "tracers": normal_values(seeds[0], (TRACERS, LEAVES_X, LEAVES_Y, NODES), 1.0, 6.0, ((1, 16), (2, 16))),
        "velocity": jnp.clip(jax.random.uniform(seeds[1], (2, LEAVES_X, LEAVES_Y), jnp.float32, -0.04, 0.04) * shard_levels(seeds[1], (2, LEAVES_X, LEAVES_Y), ((1, 16), (2, 16)), -0.4, 0.0), -0.04, 0.04),
        "inflow": draw_inflow(jax.random.fold_in(seeds[16], 71), 0),
        "leaf_solve": normal_values(seeds[3], (NODES, NODES), NODES ** -0.5, 0.375, (), jnp.float32),
        "leaf_skeleton": normal_values(seeds[4], (NODES, LEAF_SKEL), NODES ** -0.5, 0.375, (), jnp.float32),
        "leaf_lift": normal_values(seeds[5], (LEAF_SKEL, NODES), LEAF_SKEL ** -0.5, 0.75, (), jnp.float32),
        "merge_first": normal_values(seeds[6], (2 * LEAF_SKEL, LEAF_SKEL), (2 * LEAF_SKEL) ** -0.5, 0.5, (), jnp.float32),
        "merge_second": normal_values(seeds[7], (2 * LEAF_SKEL, RANK), (2 * LEAF_SKEL) ** -0.5, 0.5, (), jnp.float32),
        "merge_rest": normal_values(seeds[8], (LEVELS - 2, 2 * RANK, RANK), (2 * RANK) ** -0.5, 0.375, (), jnp.float32),
        "parent_first": normal_values(seeds[9], (LEAF_SKEL, 2 * LEAF_SKEL), LEAF_SKEL ** -0.5, 0.75, (), jnp.float32),
        "parent_second": normal_values(seeds[10], (RANK, 2 * LEAF_SKEL), RANK ** -0.5, 0.5, (), jnp.float32),
        "parent_rest": normal_values(seeds[11], (LEVELS - 2, RANK, 2 * RANK), RANK ** -0.5, 0.5, (), jnp.float32),
        "sibling_first": normal_values(seeds[12], (2 * LEAF_SKEL, 2 * LEAF_SKEL), (32 * LEAF_SKEL) ** -0.5, 0.125, (), jnp.float32),
        "sibling_second": normal_values(seeds[13], (2 * LEAF_SKEL, 2 * LEAF_SKEL), (32 * LEAF_SKEL) ** -0.5, 0.125, (), jnp.float32),
        "sibling_rest": normal_values(seeds[14], (LEVELS - 2, 2 * RANK, 2 * RANK), (32 * RANK) ** -0.5, 0.09375, (), jnp.float32),
        "root_map": normal_values(seeds[15], (RANK, RANK), RANK ** -0.5, 0.5, (), jnp.float32),
    }


highest = lax.Precision.HIGHEST


def product(left, right):
    return jnp.dot(left, right, precision=highest, preferred_element_type=jnp.float32)


def spectral_matrix(node_count):
    node_index = jnp.arange(node_count)
    points = -jnp.cos(jnp.pi * node_index.astype(jnp.float32) / (node_count - 1))
    end_weights = jnp.where((node_index == 0) | (node_index == node_count - 1), 2.0, 1.0)
    parity = jnp.where(node_index % 2 == 0, 1.0, -1.0)
    weights = (end_weights * parity).astype(jnp.float32)
    identity = jnp.eye(node_count, dtype=jnp.float32)
    offsets = points[:, None] - points[None, :] + identity
    matrix = (weights[:, None] / weights[None, :]) / offsets * (1.0 - identity)
    return matrix - jnp.diag(jnp.sum(matrix, axis=1))


def derivative_tables(node_count):
    spectral = spectral_matrix(node_count)
    identity = jnp.eye(node_count, dtype=jnp.float32)
    return jnp.concatenate([jnp.kron(spectral, identity).T, jnp.kron(identity, spectral).T], axis=1)


def side_table(node_count):
    node_index = jnp.arange(node_count * node_count)
    along_first = node_index // node_count
    along_second = node_index % node_count
    position = jnp.arange(node_count)[:, None]
    table_rows = [(along_first[None, :] == 0) & (along_second[None, :] == position),
                  (along_first[None, :] == node_count - 1) & (along_second[None, :] == position),
                  (along_second[None, :] == 0) & (along_first[None, :] == position),
                  (along_second[None, :] == node_count - 1) & (along_first[None, :] == position)]
    return jnp.concatenate(table_rows, axis=0).astype(jnp.float32)


def edge_values(tracer_field, node_count):
    node_grid = tracer_field.reshape(tracer_field.shape[:-1] + (node_count, node_count))
    return (node_grid[..., 0, :], node_grid[..., node_count - 1, :],
            node_grid[..., :, 0], node_grid[..., :, node_count - 1])


def forcing_term(tracer_field, own_edges, neighbours, velocity, inflow):
    node_count = own_edges[0].shape[-1]
    square = node_count * node_count
    gradients = product(tracer_field, derivative_tables(node_count))
    advective = velocity[0][None, :, :, None] * gradients[..., :square] + velocity[1][None, :, :, None] * gradients[..., square:]
    penalty_terms = []
    for side_index in range(4):
        strength = inflow[side_index].astype(jnp.float32) * (node_count * jnp.abs(velocity[side_index // 2]))
        penalty_terms.append(strength[None, :, :, None] * (neighbours[side_index] - own_edges[side_index]))
    penalty = product(jnp.concatenate(penalty_terms, axis=-1), side_table(node_count))
    return tracer_field - advective + penalty


def level_operators(level, tables):
    if level == 0:
        return tables[0]
    if level == 1:
        return tables[1]
    return tuple(stacked[level - 2] for stacked in tables[2])


def split_pairs(current, merge_axis):
    new_shape = current.shape[:merge_axis] + (current.shape[merge_axis] // 2, 2) + current.shape[merge_axis + 1:]
    paired = current.reshape(new_shape)
    return lax.index_in_dim(paired, 0, merge_axis + 1, False), lax.index_in_dim(paired, 1, merge_axis + 1, False)


def join_pairs(former, latter, merge_axis):
    joined = jnp.stack([former, latter], axis=merge_axis + 1)
    new_shape = list(former.shape)
    new_shape[merge_axis] = new_shape[merge_axis] * 2
    return joined.reshape(tuple(new_shape))


def ascend(current, merge_plan, start_level, tables):
    levels = []
    for offset, merge_axis in enumerate(merge_plan):
        level = start_level + offset
        former, latter = split_pairs(current, merge_axis)
        levels.append((former, latter, merge_axis, level))
        current = product(jnp.concatenate([former, latter], axis=-1), level_operators(level, tables)[0])
    return current, levels


def descend(boundary, levels, tables):
    for former, latter, merge_axis, level in reversed(levels):
        operators = level_operators(level, tables)
        joined_pair = product(boundary, operators[1]) + product(
            jnp.concatenate([former, latter], axis=-1), operators[2])
        half_width = joined_pair.shape[-1] // 2
        boundary = join_pairs(joined_pair[..., :half_width], joined_pair[..., half_width:], merge_axis)
    return boundary


def local_plan(leaf_side):
    merge_plan = []
    block_span = leaf_side
    while block_span > 1:
        merge_plan = merge_plan + [1, 2]
        block_span = block_span // 2
    return merge_plan


def cross_plan(count_first, count_second):
    merge_plan = []
    while count_first * count_second > 1:
        if count_first >= count_second:
            merge_plan.append(1)
            count_first = count_first // 2
        else:
            merge_plan.append(2)
            count_second = count_second // 2
    return merge_plan


def reference(tracers, velocity, inflow, leaf_solve, leaf_skeleton, leaf_lift, merge_first, merge_second, merge_rest,
              parent_first, parent_second, parent_rest, sibling_first, sibling_second, sibling_rest, root_map):
    merge_plan = local_plan(LEAF_SIDE) + cross_plan(N_GX, N_GY)
    tables = ((merge_first, parent_first, sibling_first), (merge_second, parent_second, sibling_second),
              (merge_rest, parent_rest, sibling_rest))

    def one_tracer(tracer_slice):
        tracer_field = tracer_slice.astype(jnp.float32)[None]
        own_edges = edge_values(tracer_field, NODE)
        zeros_first = jnp.zeros_like(own_edges[0][:, :1])
        zeros_second = jnp.zeros_like(own_edges[2][:, :, :1])
        neighbours = (jnp.concatenate([zeros_first, own_edges[1][:, :-1]], axis=1),
                      jnp.concatenate([own_edges[0][:, 1:], zeros_first], axis=1),
                      jnp.concatenate([zeros_second, own_edges[3][:, :, :-1]], axis=2),
                      jnp.concatenate([own_edges[2][:, :, 1:], zeros_second], axis=2))
        forcing = forcing_term(tracer_field, own_edges, neighbours, velocity, inflow)
        skeleton = product(forcing, leaf_skeleton)
        tree_root, levels = ascend(skeleton, merge_plan, 0, tables)
        leaf_boundary = descend(product(tree_root, root_map), levels, tables)
        updated = product(forcing, leaf_solve) + product(leaf_boundary, leaf_lift)
        return updated.astype(jnp.bfloat16)[0]

    return lax.map(one_tracer, tracers)
```

```python
import functools

import jax
import jax.numpy as jnp
import ml_dtypes
import numpy as np
from jax import lax
from jax.experimental import pallas as pl
from jax.experimental.pallas import tpu as pltpu
from jax.sharding import PartitionSpec as P

NODE = 16
SIDE = 8
BOTH = ("gx", "gy")
BF = jnp.bfloat16
F32 = jnp.float32
BITS = (16, 1, 32, 2, 64, 4, 128, 8)
PARAMS = pltpu.CompilerParams(vmem_limit_bytes=48 * 1024 * 1024)
VM = pl.BlockSpec(memory_space=pltpu.VMEM)


def derivative_pieces():
    index = np.arange(NODE)
    points = -np.cos(np.pi * index / (NODE - 1))
    weights = np.where((index == 0) | (index == NODE - 1), 2.0, 1.0) * np.where(index % 2 == 0, 1.0, -1.0)
    eye = np.eye(NODE)
    matrix = weights[:, None] / weights[None, :] / (points[:, None] - points[None, :] + eye) * (1.0 - eye)
    matrix = matrix - np.diag(matrix.sum(axis=1))
    table = np.concatenate([np.kron(matrix, eye).T, np.kron(eye, matrix).T], axis=1).astype(np.float32)
    high = table.astype(ml_dtypes.bfloat16)
    low = (table - high.astype(np.float32)).astype(ml_dtypes.bfloat16)
    return np.concatenate([high, low], axis=0)


def dot(left, right):
    return jnp.dot(left, right, preferred_element_type=F32)


def split(value):
    high = value.astype(BF)
    return high, (value - high.astype(F32)).astype(BF)


def mm(left, right):
    left_high, left_low = split(left)
    right_high, right_low = split(right)
    return dot(left_high, right_high) + dot(left_low, right_high) + dot(left_high, right_low)


def pair_up(rows, outer, inner):
    width = rows.shape[-1]
    paired = rows.reshape(outer, 2, inner, width)
    former = paired[:, 0].reshape(outer * inner, width)
    latter = paired[:, 1].reshape(outer * inner, width)
    return jnp.concatenate([former, latter], axis=-1)


def pair_down(joined, outer, inner):
    half = joined.shape[-1] // 2
    former = joined[:, :half].reshape(outer, 1, inner, half)
    latter = joined[:, half:].reshape(outer, 1, inner, half)
    return jnp.concatenate([former, latter], axis=1).reshape(outer * 2 * inner, half)


LOCAL = ((4, 64), (16, 8), (2, 32), (4, 8), (1, 16), (1, 8))


def up_kernel(u_ref, vel_ref, flow_ref, west_ref, east_ref, south_ref, north_ref, table_ref, skel_ref,
              first_ref, second_ref, rest_ref,
              forcing_ref, c0_ref, c1_ref, c2_ref, c3_ref, c4_ref, c5_ref, root_ref, turn_ref):
    ub = u_ref[...]
    u = ub.astype(F32)
    lane_j = lax.broadcasted_iota(jnp.int32, (64, SIDE), 1)
    row_j = lax.broadcasted_iota(jnp.int32, (64, SIDE), 0) % SIDE

    def column(plane):
        spread = jnp.broadcast_to(plane[:, None, :], (SIDE, SIDE, SIDE)).reshape(64, SIDE)
        return jnp.sum(jnp.where(lane_j == row_j, spread, 0.0), axis=1, keepdims=True)

    vel = [column(vel_ref[k]) for k in range(2)]
    force = [column(flow_ref[s].astype(F32)) * (NODE * jnp.abs(vel[s // 2])) for s in range(4)]
    grads = dot(ub, table_ref[:256]) + dot(ub, table_ref[256:])

    u4 = u.reshape(8, SIDE, SIDE, 256)
    before_i = jnp.concatenate([west_ref[...].astype(F32).reshape(8, 1, SIDE, 256), u4[:, :7]], axis=1).reshape(512, 256)
    after_i = jnp.concatenate([u4[:, 1:], east_ref[...].astype(F32).reshape(8, 1, SIDE, 256)], axis=1).reshape(512, 256)
    u3 = u.reshape(64, SIDE, 256)
    place = lax.broadcasted_iota(jnp.int32, (64, SIDE, 256), 1)
    before_j = jnp.where(place == 0, south_ref[...].astype(F32)[:, None, :], pltpu.roll(u3, 1, 1)).reshape(512, 256)
    after_j = jnp.where(place == 7, north_ref[...].astype(F32)[:, None, :], pltpu.roll(u3, 7, 1)).reshape(512, 256)
    lane = lax.broadcasted_iota(jnp.int32, (1, 256), 1)
    on = [lane < NODE, lane >= 256 - NODE, lane % NODE == 0, lane % NODE == NODE - 1]
    src_i = jnp.where(on[1], before_i, jnp.where(on[0], after_i, 0.0)).astype(BF)
    src_j = jnp.where(on[3], before_j, jnp.where(on[2], after_j, 0.0)).astype(BF)
    r = lax.broadcasted_iota(jnp.int32, (256, 256), 0)
    c = lax.broadcasted_iota(jnp.int32, (256, 256), 1)
    swap_i = ((r - c == 240) | (c - r == 240)).astype(F32).astype(BF)
    swap_j = (((r - c == 15) & (c % NODE == 0)) | ((c - r == 15) & (r % NODE == 0))).astype(F32).astype(BF)
    gap_i = dot(src_i, swap_i) - u
    gap_j = dot(src_j, swap_j) - u
    str_i = jnp.where(on[0], force[0], jnp.where(on[1], force[1], 0.0))
    str_j = jnp.where(on[2], force[2], jnp.where(on[3], force[3], 0.0))

    def leafwise(coefficient, field):
        return coefficient[None] * field.reshape(8, 64, 256)

    forcing = (
        u.reshape(8, 64, 256)
        - leafwise(vel[0], grads[:, :256])
        - leafwise(vel[1], grads[:, 256:])
        + leafwise(str_i, gap_i)
        + leafwise(str_j, gap_j)
    ).reshape(512, 256)
    forcing_ref[...] = forcing
    skel = skel_ref[...]
    turn_ref[...] = mm(forcing, jnp.concatenate([skel, jnp.zeros_like(skel)], axis=1))
    current = jnp.concatenate([turn_ref[pl.ds(q, 8, stride=64), :] for q in range(64)], axis=0)[:, :64]
    outs = (c0_ref, c1_ref, c2_ref, c3_ref, c4_ref, c5_ref)
    for k in range(6):
        both = pair_up(current, *LOCAL[k])
        outs[k][...] = both
        current = mm(both, first_ref[...] if k == 0 else second_ref[...] if k == 1 else rest_ref[k - 2])
    for g in range(16):
        root_ref[g] = current


def merge_all(current, weights, outs):
    for k, weight in enumerate(weights):
        outs[k][...] = current
        boxes = current.shape[0] // 8
        current = mm(pair_up(current, boxes // 2, 8), weight)
    return current


def mid_kernel(got_ref, rest_ref, s0_ref, s1_ref, s2_ref, s3_ref, root_ref):
    current = merge_all(
        got_ref[...].reshape(128, 128), [rest_ref[k] for k in range(4, 8)], (s0_ref, s1_ref, s2_ref, s3_ref)
    )
    for g in range(16):
        root_ref[g] = current


def down_kernel(got_ref, s0_ref, s1_ref, s2_ref, s3_ref, c0_ref, c1_ref, c2_ref, c3_ref, c4_ref, c5_ref, forcing_ref,
                rest_ref, pfirst_ref, psecond_ref, prest_ref, sfirst_ref, ssecond_ref, srest_ref, rootmap_ref,
                solve_ref, lift_ref, out_ref, h0_ref, h1_ref, h2_ref, h3_ref, turn_ref):
    spot = lax.axis_index("gx") * 16 + lax.axis_index("gy")
    top = merge_all(got_ref[...].reshape(128, 128), [rest_ref[k] for k in range(8, 12)], (h0_ref, h1_ref, h2_ref, h3_ref))
    boundary = mm(top, rootmap_ref[...])
    levels = (s0_ref, s1_ref, s2_ref, s3_ref, h0_ref, h1_ref, h2_ref, h3_ref)
    bit = [(spot // b) % 2 for b in BITS]
    for k in range(7, -1, -1):
        first = 4 * (k // 4)
        pair = jnp.int32(0)
        for q in range(first + 3, k, -1):
            pair = pair * 2 + bit[q]
        both = levels[k][pl.ds(pl.multiple_of(pair * 16, 16), 16), :]
        both = jnp.concatenate([both[:8], both[8:]], axis=1)
        joined = mm(boundary, prest_ref[k + 4]) + mm(both, srest_ref[k + 4])
        boundary = jnp.where(bit[k] == 1, joined[:, 128:], joined[:, :128])
    saved = (c0_ref, c1_ref, c2_ref, c3_ref, c4_ref, c5_ref)
    for k in range(5, -1, -1):
        down = pfirst_ref[...] if k == 0 else psecond_ref[...] if k == 1 else prest_ref[k - 2]
        across = sfirst_ref[...] if k == 0 else ssecond_ref[...] if k == 1 else srest_ref[k - 2]
        boundary = pair_down(mm(boundary, down) + mm(saved[k][...], across), *LOCAL[k])
    wide = jnp.concatenate([boundary, jnp.zeros_like(boundary)], axis=1)
    for q in range(64):
        turn_ref[pl.ds(q, 8, stride=64), :] = wide[8 * q : 8 * q + 8]
    updated = mm(forcing_ref[...], solve_ref[...]) + mm(turn_ref[:, :64], lift_ref[...])
    out_ref[...] = updated.astype(BF)


def groups_of(bits):
    every = sum(bits)
    groups = []
    for base in range(256):
        if base & every == 0:
            groups.append([base | sum(b for q, b in enumerate(bits) if c >> q & 1) for c in range(16)])
    return groups


def swap_roots(copies, bits):
    return lax.all_to_all(copies, BOTH, 0, 0, axis_index_groups=groups_of(bits))


def shape(*dims, dtype=F32):
    return jax.ShapeDtypeStruct(dims, dtype)


def call(kernel, outs, scratch=()):
    many = isinstance(outs, list)
    return pl.pallas_call(
        kernel,
        out_shape=outs,
        out_specs=[VM] * len(outs) if many else VM,
        scratch_shapes=list(scratch),
        compiler_params=PARAMS,
    )


def local(
    tracers,
    velocity,
    inflow,
    leaf_solve,
    leaf_skeleton,
    leaf_lift,
    merge_first,
    merge_second,
    merge_rest,
    parent_first,
    parent_second,
    parent_rest,
    sibling_first,
    sibling_second,
    sibling_rest,
    root_map,
):
    forward = [(i, i + 1) for i in range(15)]
    backward = [(i + 1, i) for i in range(15)]
    west = lax.ppermute(tracers[:, 7], "gx", forward)
    east = lax.ppermute(tracers[:, 0], "gx", backward)
    south = lax.ppermute(tracers[:, :, 7].reshape(64, 256), "gy", forward)
    north = lax.ppermute(tracers[:, :, 0].reshape(64, 256), "gy", backward)
    table = jnp.asarray(derivative_pieces())
    forcing, c0, c1, c2, c3, c4, c5, roots = call(
        up_kernel,
        [shape(512, 256), shape(256, 128), shape(128, 128), shape(64, 256), shape(32, 256), shape(16, 256),
         shape(8, 256), shape(16, 8, 128)],
        [pltpu.VMEM((512, 128), F32)],
    )(tracers.reshape(512, 256), velocity, inflow, west, east, south, north, table, leaf_skeleton,
      merge_first, merge_second, merge_rest[:4])
    got = swap_roots(roots, BITS[:4])
    s0, s1, s2, s3, roots = call(
        mid_kernel,
        [shape(128, 128), shape(64, 128), shape(32, 128), shape(16, 128), shape(16, 8, 128)],
    )(got, merge_rest)
    got = swap_roots(roots, BITS[4:])
    out = call(
        down_kernel,
        shape(512, 256, dtype=BF),
        [pltpu.VMEM((128, 128), F32), pltpu.VMEM((64, 128), F32), pltpu.VMEM((32, 128), F32),
         pltpu.VMEM((16, 128), F32), pltpu.VMEM((512, 128), F32)],
    )(got, s0, s1, s2, s3, c0, c1, c2, c3, c4, c5, forcing, merge_rest, parent_first, parent_second, parent_rest,
      sibling_first, sibling_second, sibling_rest, root_map, leaf_solve, leaf_lift)
    return out.reshape(tracers.shape)


def solution(mesh):
    whole = P()
    in_specs = (P(None, "gx", "gy", None), P(None, "gx", "gy"), P(None, "gx", "gy")) + (whole,) * 13
    out_specs = P(None, "gx", "gy", None)
    return jax.shard_map(local, mesh=mesh, in_specs=in_specs, out_specs=out_specs, check_vma=False)
```

```python
import functools

import jax
import jax.numpy as jnp
import ml_dtypes
import numpy as np
from jax import lax
from jax.experimental import pallas as pl
from jax.experimental.pallas import tpu as pltpu
from jax.sharding import PartitionSpec as P

NODE = 16
SIDE = 8
BOTH = ("gx", "gy")
BF = jnp.bfloat16
F32 = jnp.float32
BITS = (16, 1, 32, 2, 64, 4, 128, 8)
PARAMS = pltpu.CompilerParams(vmem_limit_bytes=48 * 1024 * 1024)
VM = pl.BlockSpec(memory_space=pltpu.VMEM)


def derivative_pieces():
    index = np.arange(NODE)
    points = -np.cos(np.pi * index / (NODE - 1))
    weights = np.where((index == 0) | (index == NODE - 1), 2.0, 1.0) * np.where(index % 2 == 0, 1.0, -1.0)
    eye = np.eye(NODE)
    matrix = weights[:, None] / weights[None, :] / (points[:, None] - points[None, :] + eye) * (1.0 - eye)
    matrix = matrix - np.diag(matrix.sum(axis=1))
    table = np.concatenate([np.kron(matrix, eye).T, np.kron(eye, matrix).T], axis=1).astype(np.float32)
    high = table.astype(ml_dtypes.bfloat16)
    low = (table - high.astype(np.float32)).astype(ml_dtypes.bfloat16)
    return np.concatenate([high, low], axis=0)


def dot(left, right):
    return jnp.dot(left, right, preferred_element_type=F32)


def split(value):
    high = value.astype(BF)
    return high, (value - high.astype(F32)).astype(BF)


def mm(left, right):
    left_high, left_low = split(left)
    right_high, right_low = right if isinstance(right, tuple) else split(right)
    return dot(left_high, right_high) + dot(left_low, right_high) + dot(left_high, right_low)


def mm_t(left, right):
    sides = (((1,), (1,)), ((), ()))
    left_high, left_low = split(left)
    right_high, right_low = right[0], right[1]

    def times(a, b):
        return lax.dot_general(a, b, sides, preferred_element_type=F32)

    return times(left_high, right_high) + times(left_low, right_high) + times(left_high, right_low)


def pair_up(rows, outer, inner):
    width = rows.shape[-1]
    paired = rows.reshape(outer, 2, inner, width)
    former = paired[:, 0].reshape(outer * inner, width)
    latter = paired[:, 1].reshape(outer * inner, width)
    return jnp.concatenate([former, latter], axis=-1)


def pair_down(joined, outer, inner):
    half = joined.shape[-1] // 2
    former = joined[:, :half].reshape(outer, 1, inner, half)
    latter = joined[:, half:].reshape(outer, 1, inner, half)
    return jnp.concatenate([former, latter], axis=1).reshape(outer * 2 * inner, half)


LOCAL = ((4, 64), (16, 8), (2, 32), (4, 8), (1, 16), (1, 8))


def pack_kernel(u_ref, xa_ref, xb_ref, ya_ref, yb_ref):
    even_x = lax.axis_index("gx") % 2 == 0
    even_y = lax.axis_index("gy") % 2 == 0
    u = u_ref[...].astype(F32)
    low, high = u[:, 0], u[:, SIDE - 1]
    xa_ref[...] = jnp.where(even_x, high, low).astype(BF)
    xb_ref[...] = jnp.where(even_x, low, high).astype(BF)
    low, high = u[:, :, 0], u[:, :, SIDE - 1]
    ya_ref[...] = jnp.where(even_y, high, low).astype(BF)
    yb_ref[...] = jnp.where(even_y, low, high).astype(BF)


def lane_marks():
    lane = lax.broadcasted_iota(jnp.int32, (1, 256), 1)
    return lane < NODE, lane >= 256 - NODE, lane % NODE == 0, lane % NODE == NODE - 1


def leafwise(coefficient, field):
    return (coefficient[None] * field.reshape(8, 64, 256)).reshape(512, 256)


def halo_rows(ref, turn, mark):
    return jnp.where(mark, pltpu.roll(ref[...].astype(F32).reshape(64, 256), turn, 1), 0.0)


def base_kernel(u_ref, vel_ref, flow_ref, table_ref, skel_ref, first_ref, second_ref, rest_ref, xa_ref,
                base_ref, stri_ref, strj_ref, skel_out, first_out, second_out, rest_out):
    ub = u_ref[...]
    u = ub.astype(F32)
    on = lane_marks()
    r = lax.broadcasted_iota(jnp.int32, (256, 256), 0)
    c = lax.broadcasted_iota(jnp.int32, (256, 256), 1)
    swap_i = ((r - c == 240) | (c - r == 240)).astype(F32).astype(BF)
    swap_j = (((r - c == 15) & (c % NODE == 0)) | ((c - r == 15) & (r % NODE == 0))).astype(F32).astype(BF)
    u4 = u.reshape(8, SIDE, SIDE, 256)
    even_x = lax.axis_index("gx") % 2 == 0
    beside = xa_ref[...].astype(F32).reshape(8, 1, SIDE, 256)
    before_i = jnp.concatenate([jnp.where(even_x, 0.0, beside), u4[:, :7]], axis=1).reshape(512, 256)
    after_i = jnp.concatenate([u4[:, 1:], jnp.where(even_x, beside, 0.0)], axis=1).reshape(512, 256)
    u3 = u.reshape(64, SIDE, 256)
    place = lax.broadcasted_iota(jnp.int32, (64, SIDE, 256), 1)
    before_j = jnp.where(place == 0, 0.0, pltpu.roll(u3, 1, 1)).reshape(512, 256)
    after_j = jnp.where(place == 7, 0.0, pltpu.roll(u3, 7, 1)).reshape(512, 256)
    src_i = jnp.where(on[1], before_i, jnp.where(on[0], after_i, 0.0)).astype(BF)
    src_j = jnp.where(on[3], before_j, jnp.where(on[2], after_j, 0.0)).astype(BF)
    gap_i = dot(src_i, swap_i) - u
    gap_j = dot(src_j, swap_j) - u
    lane_j = lax.broadcasted_iota(jnp.int32, (64, SIDE), 1)
    row_j = lax.broadcasted_iota(jnp.int32, (64, SIDE), 0) % SIDE

    def column(plane):
        spread = jnp.broadcast_to(plane[:, None, :], (SIDE, SIDE, SIDE)).reshape(64, SIDE)
        return jnp.sum(jnp.where(lane_j == row_j, spread, 0.0), axis=1, keepdims=True)

    vel = [column(vel_ref[k]) for k in range(2)]
    force = [column(flow_ref[s].astype(F32)) * (NODE * jnp.abs(vel[s // 2])) for s in range(4)]
    str_i = jnp.where(on[0], force[0], jnp.where(on[1], force[1], 0.0))
    str_j = jnp.where(on[2], force[2], jnp.where(on[3], force[3], 0.0))
    stri_ref[...] = str_i
    strj_ref[...] = str_j
    grads = dot(ub, table_ref[:256]) + dot(ub, table_ref[256:])
    base_ref[...] = (
        u
        - leafwise(vel[0], grads[:, :256])
        - leafwise(vel[1], grads[:, 256:])
        + leafwise(str_i, gap_i)
        + leafwise(str_j, gap_j)
    )
    skel = skel_ref[...]
    skel_out[0], skel_out[1] = split(jnp.concatenate([skel, jnp.zeros_like(skel)], axis=0))
    first_out[0], first_out[1] = split(first_ref[...])
    second_out[0], second_out[1] = split(second_ref[...])
    for k in range(4):
        rest_out[0, k], rest_out[1, k] = split(rest_ref[k])


def up_kernel(base_ref, stri_ref, strj_ref, xb_ref, ya_ref, yb_ref, skel_ref, first_ref, second_ref, rest_ref,
              forcing_ref, c0_ref, c1_ref, c2_ref, c3_ref, c4_ref, c5_ref, root_ref, turn_ref):
    even_x = lax.axis_index("gx") % 2 == 0
    even_y = lax.axis_index("gy") % 2 == 0
    on = lane_marks()

    west = jnp.where(even_x, halo_rows(xb_ref, 16, on[0]), 0.0).reshape(8, 1, SIDE, 256)
    east = jnp.where(even_x, 0.0, halo_rows(xb_ref, 240, on[1])).reshape(8, 1, SIDE, 256)
    south = jnp.where(even_y, halo_rows(yb_ref, 241, on[2]), halo_rows(ya_ref, 241, on[2]))
    north = jnp.where(even_y, halo_rows(ya_ref, 15, on[3]), halo_rows(yb_ref, 15, on[3]))
    place = lax.broadcasted_iota(jnp.int32, (64, SIDE, 256), 1)
    side_j = jnp.where(place == 0, south[:, None, :], jnp.where(place == 7, north[:, None, :], 0.0))
    inner = base_ref[...] + leafwise(strj_ref[...], side_j)
    inner = inner.reshape(8, SIDE, SIDE, 256)
    lower = stri_ref[:SIDE].reshape(1, 1, SIDE, 256)
    upper = stri_ref[7 * SIDE :].reshape(1, 1, SIDE, 256)
    forcing = jnp.concatenate(
        [inner[:, :1] + lower * west, inner[:, 1:7], inner[:, 7:] + upper * east], axis=1
    ).reshape(512, 256)
    forcing_ref[...] = forcing
    turn_ref[...] = mm_t(forcing, skel_ref)
    current = jnp.concatenate([turn_ref[pl.ds(q, 8, stride=64), :] for q in range(64)], axis=0)[:, :64]
    outs = (c0_ref, c1_ref, c2_ref, c3_ref, c4_ref, c5_ref)
    for k in range(6):
        both = pair_up(current, *LOCAL[k])
        outs[k][...] = both
        if k == 0:
            current = mm_t(both, first_ref)
        elif k == 1:
            current = mm(both, (second_ref[0], second_ref[1]))
        else:
            current = mm(both, (rest_ref[0, k - 2], rest_ref[1, k - 2]))
    for g in range(16):
        root_ref[g] = current


def merge_all(current, weights, outs):
    for k, weight in enumerate(weights):
        outs[k][...] = current
        boxes = current.shape[0] // 8
        current = mm(pair_up(current, boxes // 2, 8), weight)
    return current


def mid_kernel(got_ref, rest_ref, s0_ref, s1_ref, s2_ref, s3_ref, root_ref):
    current = merge_all(
        got_ref[...].reshape(128, 128), [rest_ref[k] for k in range(4, 8)], (s0_ref, s1_ref, s2_ref, s3_ref)
    )
    for g in range(16):
        root_ref[g] = current


def down_kernel(got_ref, s0_ref, s1_ref, s2_ref, s3_ref, c0_ref, c1_ref, c2_ref, c3_ref, c4_ref, c5_ref, forcing_ref,
                rest_ref, pfirst_ref, psecond_ref, prest_ref, sfirst_ref, ssecond_ref, srest_ref, rootmap_ref,
                solve_ref, lift_ref, out_ref, h0_ref, h1_ref, h2_ref, h3_ref, turn_ref):
    spot = lax.axis_index("gx") * 16 + lax.axis_index("gy")
    top = merge_all(got_ref[...].reshape(128, 128), [rest_ref[k] for k in range(8, 12)], (h0_ref, h1_ref, h2_ref, h3_ref))
    boundary = mm(top, rootmap_ref[...])
    levels = (s0_ref, s1_ref, s2_ref, s3_ref, h0_ref, h1_ref, h2_ref, h3_ref)
    bit = [(spot // b) % 2 for b in BITS]
    for k in range(7, -1, -1):
        first = 4 * (k // 4)
        pair = jnp.int32(0)
        for q in range(first + 3, k, -1):
            pair = pair * 2 + bit[q]
        both = levels[k][pl.ds(pl.multiple_of(pair * 16, 16), 16), :]
        both = jnp.concatenate([both[:8], both[8:]], axis=1)
        joined = mm(boundary, prest_ref[k + 4]) + mm(both, srest_ref[k + 4])
        boundary = jnp.where(bit[k] == 1, joined[:, 128:], joined[:, :128])
    saved = (c0_ref, c1_ref, c2_ref, c3_ref, c4_ref, c5_ref)
    for k in range(5, -1, -1):
        down = pfirst_ref[...] if k == 0 else psecond_ref[...] if k == 1 else prest_ref[k - 2]
        across = sfirst_ref[...] if k == 0 else ssecond_ref[...] if k == 1 else srest_ref[k - 2]
        boundary = pair_down(mm(boundary, down) + mm(saved[k][...], across), *LOCAL[k])
    wide = jnp.concatenate([boundary, jnp.zeros_like(boundary)], axis=1)
    for q in range(64):
        turn_ref[pl.ds(q, 8, stride=64), :] = wide[8 * q : 8 * q + 8]
    updated = mm(forcing_ref[...], solve_ref[...]) + mm(turn_ref[:, :64], lift_ref[...])
    out_ref[...] = updated.astype(BF)


def groups_of(bits):
    every = sum(bits)
    groups = []
    for base in range(256):
        if base & every == 0:
            groups.append([base | sum(b for q, b in enumerate(bits) if c >> q & 1) for c in range(16)])
    return groups


def swap_roots(copies, bits):
    return lax.all_to_all(copies, BOTH, 0, 0, axis_index_groups=groups_of(bits))


def shape(*dims, dtype=F32):
    return jax.ShapeDtypeStruct(dims, dtype)


def cost_of(mebibytes):
    return pl.CostEstimate(flops=0, transcendentals=0, bytes_accessed=mebibytes * 2**20)


def call(kernel, outs, scratch=(), cost=None):
    many = isinstance(outs, list)
    return pl.pallas_call(
        kernel,
        out_shape=outs,
        out_specs=[VM] * len(outs) if many else VM,
        scratch_shapes=list(scratch),
        compiler_params=PARAMS,
        cost_estimate=cost,
    )


def local(
    tracers,
    velocity,
    inflow,
    leaf_solve,
    leaf_skeleton,
    leaf_lift,
    merge_first,
    merge_second,
    merge_rest,
    parent_first,
    parent_second,
    parent_rest,
    sibling_first,
    sibling_second,
    sibling_rest,
    root_map,
):
    swap = [(i, i ^ 1) for i in range(16)]
    across = [(i, i + 1) for i in range(1, 15, 2)] + [(i + 1, i) for i in range(1, 15, 2)]
    edge = shape(8, SIDE, 256, dtype=BF)
    xa, xb, ya, yb = call(pack_kernel, [edge] * 4, cost=pl.CostEstimate(flops=10**10, transcendentals=0, bytes_accessed=2**25))(tracers)
    yb = lax.ppermute(yb, "gy", across)
    xb = lax.ppermute(xb, "gx", across)
    ya = lax.ppermute(ya, "gy", swap)
    xa = lax.ppermute(xa, "gx", swap)
    table = jnp.asarray(derivative_pieces())
    base, str_i, str_j, skel, first, second, rest = call(
        base_kernel,
        [shape(512, 256), shape(64, 256), shape(64, 256), shape(2, 128, 256, dtype=BF),
         shape(2, 64, 128, dtype=BF), shape(2, 128, 128, dtype=BF), shape(2, 4, 256, 128, dtype=BF)],
    )(tracers.reshape(512, 256), velocity, inflow, table, leaf_skeleton.T, merge_first.T, merge_second, merge_rest, xa)
    forcing, c0, c1, c2, c3, c4, c5, roots = call(
        up_kernel,
        [shape(512, 256), shape(256, 128), shape(128, 128), shape(64, 256), shape(32, 256), shape(16, 256),
         shape(8, 256), shape(16, 8, 128)],
        [pltpu.VMEM((512, 128), F32)],
    )(base, str_i, str_j, xb, ya, yb, skel, first, second, rest)
    got = swap_roots(roots, BITS[:4])
    s0, s1, s2, s3, roots = call(
        mid_kernel,
        [shape(128, 128), shape(64, 128), shape(32, 128), shape(16, 128), shape(16, 8, 128)],
    )(got, merge_rest)
    got = swap_roots(roots, BITS[4:])
    out = call(
        down_kernel,
        shape(512, 256, dtype=BF),
        [pltpu.VMEM((128, 128), F32), pltpu.VMEM((64, 128), F32), pltpu.VMEM((32, 128), F32),
         pltpu.VMEM((16, 128), F32), pltpu.VMEM((512, 128), F32)],
    )(got, s0, s1, s2, s3, c0, c1, c2, c3, c4, c5, forcing, merge_rest, parent_first, parent_second, parent_rest,
      sibling_first, sibling_second, sibling_rest, root_map, leaf_solve, leaf_lift)
    return out.reshape(tracers.shape)


def solution(mesh):
    whole = P()
    in_specs = (P(None, "gx", "gy", None), P(None, "gx", "gy"), P(None, "gx", "gy")) + (whole,) * 13
    out_specs = P(None, "gx", "gy", None)
    return jax.shard_map(local, mesh=mesh, in_specs=in_specs, out_specs=out_specs, check_vma=False)
```

```python
import functools

import jax
import jax.numpy as jnp
import ml_dtypes
import numpy as np
from jax import lax
from jax.experimental import pallas as pl
from jax.experimental.pallas import tpu as pltpu
from jax.sharding import PartitionSpec as P

NODE = 16
SIDE = 8
BOTH = ("gx", "gy")
BF = jnp.bfloat16
F32 = jnp.float32
BITS = (16, 1, 32, 2, 64, 4, 128, 8)
PARAMS = pltpu.CompilerParams(vmem_limit_bytes=48 * 1024 * 1024)
WORK = pl.CostEstimate(flops=10**10, transcendentals=0, bytes_accessed=2**25)
VM = pl.BlockSpec(memory_space=pltpu.VMEM)


def derivative_pieces():
    index = np.arange(NODE)
    points = -np.cos(np.pi * index / (NODE - 1))
    weights = np.where((index == 0) | (index == NODE - 1), 2.0, 1.0) * np.where(index % 2 == 0, 1.0, -1.0)
    eye = np.eye(NODE)
    matrix = weights[:, None] / weights[None, :] / (points[:, None] - points[None, :] + eye) * (1.0 - eye)
    matrix = matrix - np.diag(matrix.sum(axis=1))
    table = np.concatenate([np.kron(matrix, eye).T, np.kron(eye, matrix).T], axis=1).astype(np.float32)
    high = table.astype(ml_dtypes.bfloat16)
    low = (table - high.astype(np.float32)).astype(ml_dtypes.bfloat16)
    return np.concatenate([high, low], axis=0)


def dot(left, right):
    return jnp.dot(left, right, preferred_element_type=F32)


def split(value):
    high = value.astype(BF)
    return high, (value - high.astype(F32)).astype(BF)


def mm(left, right):
    left_high, left_low = split(left)
    right_high, right_low = right if isinstance(right, tuple) else split(right)
    return dot(left_high, right_high) + dot(left_low, right_high) + dot(left_high, right_low)


def mm_t(left, right):
    sides = (((1,), (1,)), ((), ()))
    left_high, left_low = split(left)
    right_high, right_low = right[0], right[1]

    def times(a, b):
        return lax.dot_general(a, b, sides, preferred_element_type=F32)

    return times(left_high, right_high) + times(left_low, right_high) + times(left_high, right_low)


def pair_up(rows, outer, inner):
    width = rows.shape[-1]
    paired = rows.reshape(outer, 2, inner, width)
    former = paired[:, 0].reshape(outer * inner, width)
    latter = paired[:, 1].reshape(outer * inner, width)
    return jnp.concatenate([former, latter], axis=-1)


def pair_down(joined, outer, inner):
    half = joined.shape[-1] // 2
    former = joined[:, :half].reshape(outer, 1, inner, half)
    latter = joined[:, half:].reshape(outer, 1, inner, half)
    return jnp.concatenate([former, latter], axis=1).reshape(outer * 2 * inner, half)


LOCAL = ((4, 64), (16, 8), (2, 32), (4, 8), (1, 16), (1, 8))


def pack_kernel(u_ref, xa_ref, xb_ref, ya_ref, yb_ref):
    even_x = lax.axis_index("gx") % 2 == 0
    even_y = lax.axis_index("gy") % 2 == 0
    u = u_ref[...].astype(F32)
    low, high = u[:, 0], u[:, SIDE - 1]
    xa_ref[...] = jnp.where(even_x, high, low).astype(BF)
    xb_ref[...] = jnp.where(even_x, low, high).astype(BF)
    low, high = u[:, :, 0], u[:, :, SIDE - 1]
    ya_ref[...] = jnp.where(even_y, high, low).astype(BF)
    yb_ref[...] = jnp.where(even_y, low, high).astype(BF)


def lane_marks():
    lane = lax.broadcasted_iota(jnp.int32, (1, 256), 1)
    return lane < NODE, lane >= 256 - NODE, lane % NODE == 0, lane % NODE == NODE - 1


def leafwise(coefficient, field):
    return (coefficient[None] * field.reshape(8, 64, 256)).reshape(512, 256)


def halo_rows(ref, turn, mark):
    return jnp.where(mark, pltpu.roll(ref[...].astype(F32).reshape(64, 256), turn, 1), 0.0)


def base_kernel(u_ref, vel_ref, flow_ref, table_ref, skel_ref, first_ref, second_ref, rest_ref, xa_ref,
                base_ref, stri_ref, strj_ref, skel_out, first_out, second_out, rest_out):
    ub = u_ref[...]
    u = ub.astype(F32)
    on = lane_marks()
    r = lax.broadcasted_iota(jnp.int32, (256, 256), 0)
    c = lax.broadcasted_iota(jnp.int32, (256, 256), 1)
    swap_i = ((r - c == 240) | (c - r == 240)).astype(F32).astype(BF)
    swap_j = (((r - c == 15) & (c % NODE == 0)) | ((c - r == 15) & (r % NODE == 0))).astype(F32).astype(BF)
    u4 = u.reshape(8, SIDE, SIDE, 256)
    even_x = lax.axis_index("gx") % 2 == 0
    beside = xa_ref[...].astype(F32).reshape(8, 1, SIDE, 256)
    before_i = jnp.concatenate([jnp.where(even_x, 0.0, beside), u4[:, :7]], axis=1).reshape(512, 256)
    after_i = jnp.concatenate([u4[:, 1:], jnp.where(even_x, beside, 0.0)], axis=1).reshape(512, 256)
    u3 = u.reshape(64, SIDE, 256)
    place = lax.broadcasted_iota(jnp.int32, (64, SIDE, 256), 1)
    before_j = jnp.where(place == 0, 0.0, pltpu.roll(u3, 1, 1)).reshape(512, 256)
    after_j = jnp.where(place == 7, 0.0, pltpu.roll(u3, 7, 1)).reshape(512, 256)
    src_i = jnp.where(on[1], before_i, jnp.where(on[0], after_i, 0.0)).astype(BF)
    src_j = jnp.where(on[3], before_j, jnp.where(on[2], after_j, 0.0)).astype(BF)
    gap_i = dot(src_i, swap_i) - u
    gap_j = dot(src_j, swap_j) - u
    lane_j = lax.broadcasted_iota(jnp.int32, (64, SIDE), 1)
    row_j = lax.broadcasted_iota(jnp.int32, (64, SIDE), 0) % SIDE

    def column(plane):
        spread = jnp.broadcast_to(plane[:, None, :], (SIDE, SIDE, SIDE)).reshape(64, SIDE)
        return jnp.sum(jnp.where(lane_j == row_j, spread, 0.0), axis=1, keepdims=True)

    vel = [column(vel_ref[k]) for k in range(2)]
    force = [column(flow_ref[s].astype(F32)) * (NODE * jnp.abs(vel[s // 2])) for s in range(4)]
    str_i = jnp.where(on[0], force[0], jnp.where(on[1], force[1], 0.0))
    str_j = jnp.where(on[2], force[2], jnp.where(on[3], force[3], 0.0))
    stri_ref[...] = str_i
    strj_ref[...] = str_j
    grads = dot(ub, table_ref[:256]) + dot(ub, table_ref[256:])
    base_ref[...] = (
        u
        - leafwise(vel[0], grads[:, :256])
        - leafwise(vel[1], grads[:, 256:])
        + leafwise(str_i, gap_i)
        + leafwise(str_j, gap_j)
    )
    skel = skel_ref[...]
    skel_out[0], skel_out[1] = split(jnp.concatenate([skel, jnp.zeros_like(skel)], axis=0))
    first_out[0], first_out[1] = split(first_ref[...])
    second_out[0], second_out[1] = split(second_ref[...])
    for k in range(4):
        rest_out[0, k], rest_out[1, k] = split(rest_ref[k])


def up_kernel(base_ref, stri_ref, strj_ref, xb_ref, ya_ref, yb_ref, skel_ref, first_ref, second_ref, rest_ref,
              forcing_ref, c0_ref, c1_ref, c2_ref, c3_ref, c4_ref, c5_ref, root_ref, turn_ref):
    even_x = lax.axis_index("gx") % 2 == 0
    even_y = lax.axis_index("gy") % 2 == 0
    on = lane_marks()

    west = jnp.where(even_x, halo_rows(xb_ref, 16, on[0]), 0.0).reshape(8, 1, SIDE, 256)
    east = jnp.where(even_x, 0.0, halo_rows(xb_ref, 240, on[1])).reshape(8, 1, SIDE, 256)
    south = jnp.where(even_y, halo_rows(yb_ref, 241, on[2]), halo_rows(ya_ref, 241, on[2]))
    north = jnp.where(even_y, halo_rows(ya_ref, 15, on[3]), halo_rows(yb_ref, 15, on[3]))
    place = lax.broadcasted_iota(jnp.int32, (64, SIDE, 256), 1)
    side_j = jnp.where(place == 0, south[:, None, :], jnp.where(place == 7, north[:, None, :], 0.0))
    inner = base_ref[...] + leafwise(strj_ref[...], side_j)
    inner = inner.reshape(8, SIDE, SIDE, 256)
    lower = stri_ref[:SIDE].reshape(1, 1, SIDE, 256)
    upper = stri_ref[7 * SIDE :].reshape(1, 1, SIDE, 256)
    forcing = jnp.concatenate(
        [inner[:, :1] + lower * west, inner[:, 1:7], inner[:, 7:] + upper * east], axis=1
    ).reshape(512, 256)
    forcing_ref[...] = forcing
    turn_ref[...] = mm_t(forcing, skel_ref)
    current = jnp.concatenate([turn_ref[pl.ds(q, 8, stride=64), :] for q in range(64)], axis=0)[:, :64]
    outs = (c0_ref, c1_ref, c2_ref, c3_ref, c4_ref, c5_ref)
    for k in range(6):
        both = pair_up(current, *LOCAL[k])
        outs[k][...] = both
        if k == 0:
            current = mm_t(both, first_ref)
        elif k == 1:
            current = mm(both, (second_ref[0], second_ref[1]))
        else:
            current = mm(both, (rest_ref[0, k - 2], rest_ref[1, k - 2]))
    for g in range(16):
        root_ref[g] = current


def merge_all(current, weights, outs):
    for k, weight in enumerate(weights):
        outs[k][...] = current
        boxes = current.shape[0] // 8
        current = mm(pair_up(current, boxes // 2, 8), weight)
    return current


def mid_kernel(got_ref, rest_ref, s0_ref, s1_ref, s2_ref, s3_ref, root_ref):
    root_ref[...] = merge_all(
        got_ref[...].reshape(128, 128), [rest_ref[k] for k in range(4, 8)], (s0_ref, s1_ref, s2_ref, s3_ref)
    )


def path_bits():
    spot = lax.axis_index("gx") * 16 + lax.axis_index("gy")
    return [(spot // b) % 2 for b in BITS]


def halves(bit, former, latter):
    return jnp.where(bit == 1, latter, former), jnp.where(bit == 1, former, latter)


def ordered(bit, own, sibling):
    return jnp.concatenate([jnp.where(bit == 1, sibling, own), jnp.where(bit == 1, own, sibling)], axis=1)


def plan_kernel(s0_ref, s1_ref, s2_ref, s3_ref, rest_ref, prest_ref, srest_ref, rootmap_ref, plan_ref, known_ref):
    bit = path_bits()

    def mine(operators, k):
        operator = operators[k + 4]
        return jnp.where(bit[k] == 1, operator[:, 128:], operator[:, :128])

    levels = (s0_ref, s1_ref, s2_ref, s3_ref)
    known = jnp.zeros((8, 128), F32)
    chain = [None, mine(prest_ref, 0)]
    for k in range(1, 8):
        chain.append(mm(mine(prest_ref, k), chain[k]))
    for k in range(4):
        pair = jnp.int32(0)
        for q in range(3, k, -1):
            pair = pair * 2 + bit[q]
        both = levels[k][pl.ds(pl.multiple_of(pair * 16, 16), 16), :]
        both = jnp.concatenate([both[:8], both[8:]], axis=1)
        term = mm(both, mine(srest_ref, k))
        known = known + (term if k == 0 else mm(term, chain[k]))
    known_ref[...] = known
    above = mm(rootmap_ref[...], chain[8])
    plan = [None] * 6
    for k in (7, 6, 5):
        full = mm(rest_ref[k + 4], above) + mm(mine(srest_ref, k), chain[k])
        above, plan[k - 2] = halves(bit[k], full[:128], full[128:])
    plan[2] = above
    lowest = mm(mine(srest_ref, 4), chain[4])
    plan[0], plan[1] = lowest[:128], lowest[128:]
    for k in range(6):
        plan_ref[0, k], plan_ref[1, k] = split(plan[k])


def z_kernel(root_ref, a_ref, b_ref, c_ref, rest_ref, both_ref, pair_ref, last_ref):
    bit = path_bits()
    both = ordered(bit[4], root_ref[...], a_ref[...])
    both_ref[...] = both
    over = ordered(bit[4], b_ref[...], c_ref[...])
    boxes = mm(jnp.concatenate([both, over], axis=0), rest_ref[8])
    operator = rest_ref[9]
    parts = mm(boxes, jnp.where(bit[5] == 1, operator[128:], operator[:128]))
    pair_ref[0] = boxes[:8]
    pair_ref[1] = parts[8:]
    last_ref[...] = mm(ordered(bit[6], parts[:8], parts[8:]), rest_ref[10])


def known_kernel(c0_ref, c1_ref, c2_ref, c3_ref, c4_ref, c5_ref, forcing_ref, pfirst_ref, psecond_ref, prest_ref,
                 sfirst_ref, ssecond_ref, srest_ref, solve_ref, lift_ref, after_ref,
                 part_ref, pfirst_out, psecond_out, prest_out, lift_out, turn_ref):
    pfirst_out[0], pfirst_out[1] = split(pfirst_ref[...])
    psecond_out[0], psecond_out[1] = split(psecond_ref[...])
    for k in range(4):
        prest_out[0, k], prest_out[1, k] = split(prest_ref[k])
    lift_out[0], lift_out[1] = split(lift_ref[...])
    downs = [pfirst_out, psecond_out] + [prest_out.at[:, k] for k in range(4)]
    saved = (c0_ref, c1_ref, c2_ref, c3_ref, c4_ref, c5_ref)
    boundary = None
    for k in range(5, -1, -1):
        across = sfirst_ref[...] if k == 0 else ssecond_ref[...] if k == 1 else srest_ref[k - 2]
        joined = mm(saved[k][...], across)
        if boundary is not None:
            joined = joined + mm(boundary, (downs[k][0], downs[k][1]))
        boundary = pair_down(joined, *LOCAL[k])
    wide = jnp.concatenate([boundary, jnp.zeros_like(boundary)], axis=1)
    for q in range(64):
        turn_ref[pl.ds(q, 8, stride=64), :] = wide[8 * q : 8 * q + 8]
    part_ref[...] = mm(forcing_ref[...], solve_ref[...]) + mm(turn_ref[:, :64], (lift_out[0], lift_out[1]))


def last_kernel(both_ref, pair_ref, near_ref, far_ref, farther_ref, plan_ref, known_ref,
                part_ref, pfirst_ref, psecond_ref, prest_ref, lift_ref, out_ref, turn_ref):
    sources = [both_ref[...], pair_ref[0], near_ref[0], pair_ref[1] + near_ref[1], far_ref[...] + farther_ref[...]]
    gathered = jnp.concatenate(sources, axis=1)
    plan = plan_ref[...].reshape(2, 768, 128)
    boundary = known_ref[...] + mm(gathered, (plan[0], plan[1]))
    for k in range(5, 1, -1):
        boundary = pair_down(mm(boundary, (prest_ref[0, k - 2], prest_ref[1, k - 2])), *LOCAL[k])
    boundary = pair_down(mm(boundary, (psecond_ref[0], psecond_ref[1])), *LOCAL[1])
    boundary = pair_down(mm(boundary, (pfirst_ref[0], pfirst_ref[1])), *LOCAL[0])
    wide = jnp.concatenate([boundary, jnp.zeros_like(boundary)], axis=1)
    for q in range(64):
        turn_ref[pl.ds(q, 8, stride=64), :] = wide[8 * q : 8 * q + 8]
    out_ref[...] = (part_ref[...] + mm(turn_ref[:, :64], (lift_ref[0], lift_ref[1]))).astype(BF)


def groups_of(bits):
    every = sum(bits)
    groups = []
    for base in range(256):
        if base & every == 0:
            groups.append([base | sum(b for q, b in enumerate(bits) if c >> q & 1) for c in range(16)])
    return groups


def swap_roots(copies, bits):
    return lax.all_to_all(copies, BOTH, 0, 0, axis_index_groups=groups_of(bits))


def swap(value, mask):
    return lax.ppermute(value, BOTH, [(i, i ^ mask) for i in range(256)])


def shape(*dims, dtype=F32):
    return jax.ShapeDtypeStruct(dims, dtype)


def call(kernel, outs, scratch=(), cost=None):
    many = isinstance(outs, list)
    return pl.pallas_call(
        kernel,
        out_shape=outs,
        out_specs=[VM] * len(outs) if many else VM,
        scratch_shapes=list(scratch),
        compiler_params=PARAMS,
        cost_estimate=cost,
    )


def local(
    tracers,
    velocity,
    inflow,
    leaf_solve,
    leaf_skeleton,
    leaf_lift,
    merge_first,
    merge_second,
    merge_rest,
    parent_first,
    parent_second,
    parent_rest,
    sibling_first,
    sibling_second,
    sibling_rest,
    root_map,
):
    beside = [(i, i ^ 1) for i in range(16)]
    across = [(i, i + 1) for i in range(1, 15, 2)] + [(i + 1, i) for i in range(1, 15, 2)]
    edge = shape(8, SIDE, 256, dtype=BF)
    xa, xb, ya, yb = call(pack_kernel, [edge] * 4, cost=WORK)(tracers)
    yb = lax.ppermute(yb, "gy", across)
    xb = lax.ppermute(xb, "gx", across)
    ya = lax.ppermute(ya, "gy", beside)
    xa = lax.ppermute(xa, "gx", beside)
    table = jnp.asarray(derivative_pieces())
    base, str_i, str_j, skel, first, second, rest = call(
        base_kernel,
        [shape(512, 256), shape(64, 256), shape(64, 256), shape(2, 128, 256, dtype=BF),
         shape(2, 64, 128, dtype=BF), shape(2, 128, 128, dtype=BF), shape(2, 4, 256, 128, dtype=BF)],
    )(tracers.reshape(512, 256), velocity, inflow, table, leaf_skeleton.T, merge_first.T, merge_second, merge_rest, xa)
    forcing, c0, c1, c2, c3, c4, c5, roots = call(
        up_kernel,
        [shape(512, 256), shape(256, 128), shape(128, 128), shape(64, 256), shape(32, 256), shape(16, 256),
         shape(8, 256), shape(16, 8, 128)],
        [pltpu.VMEM((512, 128), F32)],
    )(base, str_i, str_j, xb, ya, yb, skel, first, second, rest)
    got = swap_roots(roots, BITS[:4])
    s0, s1, s2, s3, root = call(
        mid_kernel,
        [shape(128, 128), shape(64, 128), shape(32, 128), shape(16, 128), shape(8, 128)],
    )(got, merge_rest)
    third, second_z, first_z = swap(root, 192), swap(root, 128), swap(root, 64)
    plan, known = call(plan_kernel, [shape(2, 6, 128, 128, dtype=BF), shape(8, 128)], cost=WORK)(
        s0, s1, s2, s3, merge_rest, parent_rest, sibling_rest, root_map)
    both, pair, last = call(z_kernel, [shape(8, 256), shape(2, 8, 128), shape(8, 128)])(
        root, first_z, second_z, third, merge_rest)
    farther, far, near = swap(last, 12), swap(last, 8), swap(pair, 4)
    part, pfirst, psecond, prest, lift = call(
        known_kernel,
        [shape(512, 256), shape(2, 64, 128, dtype=BF), shape(2, 128, 128, dtype=BF), shape(2, 4, 128, 256, dtype=BF),
         shape(2, 64, 256, dtype=BF)],
        [pltpu.VMEM((512, 128), F32)],
        cost=WORK,
    )(c0, c1, c2, c3, c4, c5, forcing, parent_first, parent_second, parent_rest, sibling_first, sibling_second,
      sibling_rest, leaf_solve, leaf_lift, last)
    out = call(last_kernel, shape(512, 256, dtype=BF), [pltpu.VMEM((512, 128), F32)])(
        both, pair, near, far, farther, plan, known, part, pfirst, psecond, prest, lift)
    return out.reshape(tracers.shape)


def solution(mesh):
    whole = P()
    in_specs = (P(None, "gx", "gy", None), P(None, "gx", "gy"), P(None, "gx", "gy")) + (whole,) * 13
    out_specs = P(None, "gx", "gy", None)
    return jax.shard_map(local, mesh=mesh, in_specs=in_specs, out_specs=out_specs, check_vma=False)
```

```python
import functools

import jax
import jax.numpy as jnp
import ml_dtypes
import numpy as np
from jax import lax
from jax.experimental import pallas as pl
from jax.experimental.pallas import tpu as pltpu
from jax.sharding import PartitionSpec as P

NODE = 16
SIDE = 8
BOTH = ("gx", "gy")
BF = jnp.bfloat16
F32 = jnp.float32
BITS = (16, 1, 32, 2, 64, 4, 128, 8)
PARAMS = pltpu.CompilerParams(vmem_limit_bytes=48 * 1024 * 1024)
WORK = pl.CostEstimate(flops=10**10, transcendentals=0, bytes_accessed=2**25)
VM = pl.BlockSpec(memory_space=pltpu.VMEM)


def derivative_pieces():
    index = np.arange(NODE)
    points = -np.cos(np.pi * index / (NODE - 1))
    weights = np.where((index == 0) | (index == NODE - 1), 2.0, 1.0) * np.where(index % 2 == 0, 1.0, -1.0)
    eye = np.eye(NODE)
    matrix = weights[:, None] / weights[None, :] / (points[:, None] - points[None, :] + eye) * (1.0 - eye)
    matrix = matrix - np.diag(matrix.sum(axis=1))
    table = np.concatenate([np.kron(matrix, eye).T, np.kron(eye, matrix).T], axis=1).astype(np.float32)
    high = table.astype(ml_dtypes.bfloat16)
    low = (table - high.astype(np.float32)).astype(ml_dtypes.bfloat16)
    return np.concatenate([high, low], axis=0)


def dot(left, right):
    return jnp.dot(left, right, preferred_element_type=F32)


def split(value):
    high = value.astype(BF)
    return high, (value - high.astype(F32)).astype(BF)


def mm(left, right):
    left_high, left_low = split(left)
    right_high, right_low = right if isinstance(right, tuple) else split(right)
    return dot(left_high, right_high) + dot(left_low, right_high) + dot(left_high, right_low)


def mm_t(left, right):
    sides = (((1,), (1,)), ((), ()))
    left_high, left_low = split(left)
    right_high, right_low = right[0], right[1]

    def times(a, b):
        return lax.dot_general(a, b, sides, preferred_element_type=F32)

    return times(left_high, right_high) + times(left_low, right_high) + times(left_high, right_low)


def pair_up(rows, outer, inner):
    width = rows.shape[-1]
    paired = rows.reshape(outer, 2, inner, width)
    former = paired[:, 0].reshape(outer * inner, width)
    latter = paired[:, 1].reshape(outer * inner, width)
    return jnp.concatenate([former, latter], axis=-1)


def pair_down(joined, outer, inner):
    half = joined.shape[-1] // 2
    former = joined[:, :half].reshape(outer, 1, inner, half)
    latter = joined[:, half:].reshape(outer, 1, inner, half)
    return jnp.concatenate([former, latter], axis=1).reshape(outer * 2 * inner, half)


LOCAL = ((4, 64), (16, 8), (2, 32), (4, 8), (1, 16), (1, 8))


def pack_kernel(u_ref, yb_ref, xb_ref, ya_ref, xa_ref):
    even_x = lax.axis_index("gx") % 2 == 0
    even_y = lax.axis_index("gy") % 2 == 0
    u = u_ref[...].astype(F32)
    low, high = u[:, 0], u[:, SIDE - 1]
    xa_ref[...] = jnp.where(even_x, high, low).astype(BF)
    xb_ref[...] = jnp.where(even_x, low, high).astype(BF)
    low, high = u[:, :, 0], u[:, :, SIDE - 1]
    ya_ref[...] = jnp.where(even_y, high, low).astype(BF)
    yb_ref[...] = jnp.where(even_y, low, high).astype(BF)


def lane_marks():
    lane = lax.broadcasted_iota(jnp.int32, (1, 256), 1)
    return lane < NODE, lane >= 256 - NODE, lane % NODE == 0, lane % NODE == NODE - 1


def leafwise(coefficient, field):
    return (coefficient[None] * field.reshape(8, 64, 256)).reshape(512, 256)


def halo_rows(ref, turn, mark):
    return jnp.where(mark, pltpu.roll(ref[...].astype(F32).reshape(64, 256), turn, 1), 0.0)


def base_kernel(u_ref, vel_ref, flow_ref, table_ref, skel_ref, first_ref, second_ref, rest_ref, xa_ref,
                base_ref, stri_ref, strj_ref, skel_out, first_out, second_out, rest_out):
    ub = u_ref[...]
    u = ub.astype(F32)
    on = lane_marks()
    r = lax.broadcasted_iota(jnp.int32, (256, 256), 0)
    c = lax.broadcasted_iota(jnp.int32, (256, 256), 1)
    swap_i = ((r - c == 240) | (c - r == 240)).astype(F32).astype(BF)
    swap_j = (((r - c == 15) & (c % NODE == 0)) | ((c - r == 15) & (r % NODE == 0))).astype(F32).astype(BF)
    u4 = u.reshape(8, SIDE, SIDE, 256)
    even_x = lax.axis_index("gx") % 2 == 0
    beside = xa_ref[...].astype(F32).reshape(8, 1, SIDE, 256)
    before_i = jnp.concatenate([jnp.where(even_x, 0.0, beside), u4[:, :7]], axis=1).reshape(512, 256)
    after_i = jnp.concatenate([u4[:, 1:], jnp.where(even_x, beside, 0.0)], axis=1).reshape(512, 256)
    u3 = u.reshape(64, SIDE, 256)
    place = lax.broadcasted_iota(jnp.int32, (64, SIDE, 256), 1)
    before_j = jnp.where(place == 0, 0.0, pltpu.roll(u3, 1, 1)).reshape(512, 256)
    after_j = jnp.where(place == 7, 0.0, pltpu.roll(u3, 7, 1)).reshape(512, 256)
    src_i = jnp.where(on[1], before_i, jnp.where(on[0], after_i, 0.0)).astype(BF)
    src_j = jnp.where(on[3], before_j, jnp.where(on[2], after_j, 0.0)).astype(BF)
    gap_i = dot(src_i, swap_i) - u
    gap_j = dot(src_j, swap_j) - u
    lane_j = lax.broadcasted_iota(jnp.int32, (64, SIDE), 1)
    row_j = lax.broadcasted_iota(jnp.int32, (64, SIDE), 0) % SIDE

    def column(plane):
        spread = jnp.broadcast_to(plane[:, None, :], (SIDE, SIDE, SIDE)).reshape(64, SIDE)
        return jnp.sum(jnp.where(lane_j == row_j, spread, 0.0), axis=1, keepdims=True)

    vel = [column(vel_ref[k]) for k in range(2)]
    force = [column(flow_ref[s].astype(F32)) * (NODE * jnp.abs(vel[s // 2])) for s in range(4)]
    str_i = jnp.where(on[0], force[0], jnp.where(on[1], force[1], 0.0))
    str_j = jnp.where(on[2], force[2], jnp.where(on[3], force[3], 0.0))
    stri_ref[...] = str_i
    strj_ref[...] = str_j
    grads = dot(ub, table_ref[:256]) + dot(ub, table_ref[256:])
    base_ref[...] = (
        u
        - leafwise(vel[0], grads[:, :256])
        - leafwise(vel[1], grads[:, 256:])
        + leafwise(str_i, gap_i)
        + leafwise(str_j, gap_j)
    )
    skel = skel_ref[...]
    skel_out[0], skel_out[1] = split(jnp.concatenate([skel, jnp.zeros_like(skel)], axis=0))
    first_out[0], first_out[1] = split(first_ref[...])
    second_out[0], second_out[1] = split(second_ref[...])
    for k in range(4):
        rest_out[0, k], rest_out[1, k] = split(rest_ref[k])


def up_kernel(base_ref, stri_ref, strj_ref, yb_ref, xb_ref, ya_ref, skel_ref, first_ref, second_ref, rest_ref,
              forcing_ref, c0_ref, c1_ref, c2_ref, c3_ref, c4_ref, c5_ref, root_ref, turn_ref):
    even_x = lax.axis_index("gx") % 2 == 0
    even_y = lax.axis_index("gy") % 2 == 0
    on = lane_marks()

    west = jnp.where(even_x, halo_rows(xb_ref, 16, on[0]), 0.0).reshape(8, 1, SIDE, 256)
    east = jnp.where(even_x, 0.0, halo_rows(xb_ref, 240, on[1])).reshape(8, 1, SIDE, 256)
    south = jnp.where(even_y, halo_rows(yb_ref, 241, on[2]), halo_rows(ya_ref, 241, on[2]))
    north = jnp.where(even_y, halo_rows(ya_ref, 15, on[3]), halo_rows(yb_ref, 15, on[3]))
    place = lax.broadcasted_iota(jnp.int32, (64, SIDE, 256), 1)
    side_j = jnp.where(place == 0, south[:, None, :], jnp.where(place == 7, north[:, None, :], 0.0))
    inner = base_ref[...] + leafwise(strj_ref[...], side_j)
    inner = inner.reshape(8, SIDE, SIDE, 256)
    lower = stri_ref[:SIDE].reshape(1, 1, SIDE, 256)
    upper = stri_ref[7 * SIDE :].reshape(1, 1, SIDE, 256)
    forcing = jnp.concatenate(
        [inner[:, :1] + lower * west, inner[:, 1:7], inner[:, 7:] + upper * east], axis=1
    ).reshape(512, 256)
    forcing_ref[...] = forcing
    turn_ref[...] = mm_t(forcing, skel_ref)
    current = jnp.concatenate([turn_ref[pl.ds(q, 8, stride=64), :] for q in range(64)], axis=0)[:, :64]
    outs = (c0_ref, c1_ref, c2_ref, c3_ref, c4_ref, c5_ref)
    for k in range(6):
        both = pair_up(current, *LOCAL[k])
        outs[k][...] = both
        if k == 0:
            current = mm_t(both, first_ref)
        elif k == 1:
            current = mm(both, (second_ref[0], second_ref[1]))
        else:
            current = mm(both, (rest_ref[0, k - 2], rest_ref[1, k - 2]))
    for g in range(16):
        root_ref[g] = current


def merge_all(current, weights, outs):
    for k, weight in enumerate(weights):
        outs[k][...] = current
        boxes = current.shape[0] // 8
        current = mm(pair_up(current, boxes // 2, 8), weight)
    return current


def mid_kernel(got_ref, rest_ref, s0_ref, s1_ref, s2_ref, s3_ref, root_ref):
    root_ref[...] = merge_all(
        got_ref[...].reshape(128, 128), [rest_ref[k] for k in range(4, 8)], (s0_ref, s1_ref, s2_ref, s3_ref)
    )


def path_bits():
    spot = lax.axis_index("gx") * 16 + lax.axis_index("gy")
    return [(spot // b) % 2 for b in BITS]


def halves(bit, former, latter):
    return jnp.where(bit == 1, latter, former), jnp.where(bit == 1, former, latter)


def ordered(bit, own, sibling):
    return jnp.concatenate([jnp.where(bit == 1, sibling, own), jnp.where(bit == 1, own, sibling)], axis=1)


def plan_kernel(s0_ref, s1_ref, s2_ref, s3_ref, rest_ref, prest_ref, srest_ref, rootmap_ref, plan_ref, known_ref):
    bit = path_bits()

    def mine(operators, k):
        operator = operators[k + 4]
        return jnp.where(bit[k] == 1, operator[:, 128:], operator[:, :128])

    levels = (s0_ref, s1_ref, s2_ref, s3_ref)
    known = jnp.zeros((8, 128), F32)
    step = [mine(prest_ref, k) for k in range(8)]
    twice = [mm(step[k + 1], step[k]) for k in (2, 4, 6)]
    chain = [None, step[0], mm(step[1], step[0])]
    for k in (2, 4):
        chain.append(mm(step[k], chain[k]))
        chain.append(mm(twice[k // 2 - 1], chain[k]))
    chain.append(mm(step[6], chain[6]))
    for k in range(4):
        pair = jnp.int32(0)
        for q in range(3, k, -1):
            pair = pair * 2 + bit[q]
        both = levels[k][pl.ds(pl.multiple_of(pair * 16, 16), 16), :]
        both = jnp.concatenate([both[:8], both[8:]], axis=1)
        term = mm(both, mine(srest_ref, k))
        known = known + (term if k == 0 else mm(term, chain[k]))
    known_ref[...] = known
    above = mm(mm(rootmap_ref[...], twice[2]), chain[6])
    plan = [None] * 6
    for k in (7, 6, 5):
        full = mm(rest_ref[k + 4], above) + mm(mine(srest_ref, k), chain[k])
        above, plan[k - 2] = halves(bit[k], full[:128], full[128:])
    plan[2] = above
    lowest = mm(mine(srest_ref, 4), chain[4])
    plan[0], plan[1] = lowest[:128], lowest[128:]
    for k in range(6):
        plan_ref[0, k], plan_ref[1, k] = split(plan[k])


def z_kernel(root_ref, b_ref, c_ref, a_ref, rest_ref, both_ref, pair_ref, last_ref):
    bit = path_bits()
    both = ordered(bit[4], root_ref[...], a_ref[...])
    both_ref[...] = both
    over = ordered(bit[4], b_ref[...], c_ref[...])
    boxes = mm(jnp.concatenate([both, over], axis=0), rest_ref[8])
    operator = rest_ref[9]
    parts = mm(boxes, jnp.where(bit[5] == 1, operator[128:], operator[:128]))
    pair_ref[0] = boxes[:8]
    pair_ref[1] = parts[8:]
    last_ref[...] = mm(ordered(bit[6], parts[:8], parts[8:]), rest_ref[10])


def known_kernel(c0_ref, c1_ref, c2_ref, c3_ref, c4_ref, c5_ref, forcing_ref, pfirst_ref, psecond_ref, prest_ref,
                 sfirst_ref, ssecond_ref, srest_ref, solve_ref, lift_ref, after_ref,
                 part_ref, t0_ref, t1_ref, t2_ref, t3_ref, t4_ref, t5_ref, pfirst_out, psecond_out, prest_out, lift_out):
    pfirst_out[0], pfirst_out[1] = split(pfirst_ref[...])
    psecond_out[0], psecond_out[1] = split(psecond_ref[...])
    for k in range(4):
        prest_out[0, k], prest_out[1, k] = split(prest_ref[k])
    lift_out[0], lift_out[1] = split(lift_ref[...])
    saved = (c0_ref, c1_ref, c2_ref, c3_ref, c4_ref, c5_ref)
    terms = (t0_ref, t1_ref, t2_ref, t3_ref, t4_ref, t5_ref)
    for k in range(6):
        across = sfirst_ref[...] if k == 0 else ssecond_ref[...] if k == 1 else srest_ref[k - 2]
        terms[k][...] = mm(saved[k][...], across)
    part_ref[...] = mm(forcing_ref[...], solve_ref[...])


def last_kernel(both_ref, pair_ref, near_ref, far_ref, farther_ref, plan_ref, known_ref, part_ref,
                t0_ref, t1_ref, t2_ref, t3_ref, t4_ref, t5_ref,
                pfirst_ref, psecond_ref, prest_ref, lift_ref, out_ref, turn_ref):
    sources = [both_ref[...], pair_ref[0], near_ref[0], pair_ref[1] + near_ref[1], far_ref[...] + farther_ref[...]]
    gathered = jnp.concatenate(sources, axis=1)
    plan = plan_ref[...].reshape(2, 768, 128)
    boundary = known_ref[...] + mm(gathered, (plan[0], plan[1]))
    terms = (t0_ref, t1_ref, t2_ref, t3_ref, t4_ref, t5_ref)
    downs = [pfirst_ref, psecond_ref] + [prest_ref.at[:, k] for k in range(4)]
    for k in range(5, -1, -1):
        boundary = pair_down(terms[k][...] + mm(boundary, (downs[k][0], downs[k][1])), *LOCAL[k])
    wide = jnp.concatenate([boundary, jnp.zeros_like(boundary)], axis=1)
    for q in range(64):
        turn_ref[pl.ds(q, 8, stride=64), :] = wide[8 * q : 8 * q + 8]
    out_ref[...] = (part_ref[...] + mm(turn_ref[:, :64], (lift_ref[0], lift_ref[1]))).astype(BF)


def groups_of(bits):
    every = sum(bits)
    groups = []
    for base in range(256):
        if base & every == 0:
            groups.append([base | sum(b for q, b in enumerate(bits) if c >> q & 1) for c in range(16)])
    return groups


def swap_roots(copies, bits):
    return lax.all_to_all(copies, BOTH, 0, 0, axis_index_groups=groups_of(bits))


def swap(value, mask):
    return lax.ppermute(value, BOTH, [(i, i ^ mask) for i in range(256)])


def shape(*dims, dtype=F32):
    return jax.ShapeDtypeStruct(dims, dtype)


def call(kernel, outs, scratch=(), cost=None):
    many = isinstance(outs, list)
    return pl.pallas_call(
        kernel,
        out_shape=outs,
        out_specs=[VM] * len(outs) if many else VM,
        scratch_shapes=list(scratch),
        compiler_params=PARAMS,
        cost_estimate=cost,
    )


def local(
    tracers,
    velocity,
    inflow,
    leaf_solve,
    leaf_skeleton,
    leaf_lift,
    merge_first,
    merge_second,
    merge_rest,
    parent_first,
    parent_second,
    parent_rest,
    sibling_first,
    sibling_second,
    sibling_rest,
    root_map,
):
    beside = [(i, i ^ 1) for i in range(16)]
    across = [(i, i + 1) for i in range(1, 15, 2)] + [(i + 1, i) for i in range(1, 15, 2)]
    edge = shape(8, SIDE, 256, dtype=BF)
    yb, xb, ya, xa = call(pack_kernel, [edge] * 4, cost=WORK)(tracers)
    xa = lax.ppermute(xa, "gx", beside)
    ya = lax.ppermute(ya, "gy", beside)
    xb = lax.ppermute(xb, "gx", across)
    yb = lax.ppermute(yb, "gy", across)
    table = jnp.asarray(derivative_pieces())
    base, str_i, str_j, skel, first, second, rest = call(
        base_kernel,
        [shape(512, 256), shape(64, 256), shape(64, 256), shape(2, 128, 256, dtype=BF),
         shape(2, 64, 128, dtype=BF), shape(2, 128, 128, dtype=BF), shape(2, 4, 256, 128, dtype=BF)],
    )(tracers.reshape(512, 256), velocity, inflow, table, leaf_skeleton.T, merge_first.T, merge_second, merge_rest, xa)
    forcing, c0, c1, c2, c3, c4, c5, roots = call(
        up_kernel,
        [shape(512, 256), shape(256, 128), shape(128, 128), shape(64, 256), shape(32, 256), shape(16, 256),
         shape(8, 256), shape(16, 8, 128)],
        [pltpu.VMEM((512, 128), F32)],
    )(base, str_i, str_j, yb, xb, ya, skel, first, second, rest)
    got = swap_roots(roots, BITS[:4])
    s0, s1, s2, s3, root = call(
        mid_kernel,
        [shape(128, 128), shape(64, 128), shape(32, 128), shape(16, 128), shape(8, 128)],
    )(got, merge_rest)
    first_z, third, second_z = swap(root, 64), swap(root, 192), swap(root, 128)
    plan, known = call(plan_kernel, [shape(2, 6, 128, 128, dtype=BF), shape(8, 128)], cost=WORK)(
        s0, s1, s2, s3, merge_rest, parent_rest, sibling_rest, root_map)
    both, pair, last = call(z_kernel, [shape(8, 256), shape(2, 8, 128), shape(8, 128)])(
        root, second_z, third, first_z, merge_rest)
    farther, far, near = swap(last, 12), swap(last, 8), swap(pair, 4)
    part, *rest_of = call(
        known_kernel,
        [shape(512, 256), shape(256, 128), shape(128, 128), shape(64, 256), shape(32, 256), shape(16, 256), shape(8, 256),
         shape(2, 64, 128, dtype=BF), shape(2, 128, 128, dtype=BF), shape(2, 4, 128, 256, dtype=BF),
         shape(2, 64, 256, dtype=BF)],
        cost=WORK,
    )(c0, c1, c2, c3, c4, c5, forcing, parent_first, parent_second, parent_rest, sibling_first, sibling_second,
      sibling_rest, leaf_solve, leaf_lift, last)
    out = call(last_kernel, shape(512, 256, dtype=BF), [pltpu.VMEM((512, 128), F32)])(
        both, pair, near, far, farther, plan, known, part, *rest_of)
    return out.reshape(tracers.shape)


def solution(mesh):
    whole = P()
    in_specs = (P(None, "gx", "gy", None), P(None, "gx", "gy"), P(None, "gx", "gy")) + (whole,) * 13
    out_specs = P(None, "gx", "gy", None)
    return jax.shard_map(local, mesh=mesh, in_specs=in_specs, out_specs=out_specs, check_vma=False)
```

```python
import functools

import jax
import jax.numpy as jnp
import ml_dtypes
import numpy as np
from jax import lax
from jax.experimental import pallas as pl
from jax.experimental.pallas import tpu as pltpu
from jax.sharding import PartitionSpec as P

NODE = 16
SIDE = 8
BOTH = ("gx", "gy")
BF = jnp.bfloat16
F32 = jnp.float32
BITS = (16, 1, 32, 2, 64, 4, 128, 8)
PARAMS = pltpu.CompilerParams(vmem_limit_bytes=32 * 1024 * 1024)
WORK = pl.CostEstimate(flops=10**10, transcendentals=0, bytes_accessed=2**25)
VM = pl.BlockSpec(memory_space=pltpu.VMEM)


def derivative_pieces():
    index = np.arange(NODE)
    points = -np.cos(np.pi * index / (NODE - 1))
    weights = np.where((index == 0) | (index == NODE - 1), 2.0, 1.0) * np.where(index % 2 == 0, 1.0, -1.0)
    eye = np.eye(NODE)
    matrix = weights[:, None] / weights[None, :] / (points[:, None] - points[None, :] + eye) * (1.0 - eye)
    matrix = matrix - np.diag(matrix.sum(axis=1))
    table = np.concatenate([np.kron(matrix, eye).T, np.kron(eye, matrix).T], axis=1).astype(np.float32)
    high = table.astype(ml_dtypes.bfloat16)
    low = (table - high.astype(np.float32)).astype(ml_dtypes.bfloat16)
    return np.concatenate([high, low], axis=0)


def dot(left, right):
    return jnp.dot(left, right, preferred_element_type=F32)


def split(value):
    high = value.astype(BF)
    return high, (value - high.astype(F32)).astype(BF)


def mm(left, right):
    left_high, left_low = split(left)
    right_high, right_low = right if isinstance(right, tuple) else split(right)
    return dot(left_high, right_high) + dot(left_low, right_high) + dot(left_high, right_low)


def mm_t(left, right):
    sides = (((1,), (1,)), ((), ()))
    left_high, left_low = split(left)
    right_high, right_low = right[0], right[1]

    def times(a, b):
        return lax.dot_general(a, b, sides, preferred_element_type=F32)

    return times(left_high, right_high) + times(left_low, right_high) + times(left_high, right_low)


def pair_up(rows, outer, inner):
    width = rows.shape[-1]
    paired = rows.reshape(outer, 2, inner, width)
    former = paired[:, 0].reshape(outer * inner, width)
    latter = paired[:, 1].reshape(outer * inner, width)
    return jnp.concatenate([former, latter], axis=-1)


def pair_down(joined, outer, inner):
    half = joined.shape[-1] // 2
    former = joined[:, :half].reshape(outer, 1, inner, half)
    latter = joined[:, half:].reshape(outer, 1, inner, half)
    return jnp.concatenate([former, latter], axis=1).reshape(outer * 2 * inner, half)


LOCAL = ((4, 64), (16, 8), (2, 32), (4, 8), (1, 16), (1, 8))


def pack_kernel(u_ref, yb_ref, xb_ref, ya_ref, xa_ref):
    even_x = lax.axis_index("gx") % 2 == 0
    even_y = lax.axis_index("gy") % 2 == 0
    u = u_ref[...].astype(F32)
    low, high = u[:, 0], u[:, SIDE - 1]
    xa_ref[...] = jnp.where(even_x, high, low).astype(BF)
    xb_ref[...] = jnp.where(even_x, low, high).astype(BF)
    low, high = u[:, :, 0], u[:, :, SIDE - 1]
    ya_ref[...] = jnp.where(even_y, high, low).astype(BF)
    yb_ref[...] = jnp.where(even_y, low, high).astype(BF)


def lane_marks():
    lane = lax.broadcasted_iota(jnp.int32, (1, 256), 1)
    return lane < NODE, lane >= 256 - NODE, lane % NODE == 0, lane % NODE == NODE - 1


def leafwise(coefficient, field):
    return (coefficient[None] * field.reshape(8, 64, 256)).reshape(512, 256)


def halo_rows(ref, turn, mark):
    return jnp.where(mark, pltpu.roll(ref[...].astype(F32).reshape(64, 256), turn, 1), 0.0)


def base_kernel(u_ref, vel_ref, flow_ref, table_ref, skel_ref, first_ref, second_ref, rest_ref, xa_ref,
                base_ref, stri_ref, strj_ref, skel_out, first_out, second_out, rest_out):
    ub = u_ref[...]
    u = ub.astype(F32)
    on = lane_marks()
    r = lax.broadcasted_iota(jnp.int32, (256, 256), 0)
    c = lax.broadcasted_iota(jnp.int32, (256, 256), 1)
    swap_i = ((r - c == 240) | (c - r == 240)).astype(F32).astype(BF)
    swap_j = (((r - c == 15) & (c % NODE == 0)) | ((c - r == 15) & (r % NODE == 0))).astype(F32).astype(BF)
    u4 = u.reshape(8, SIDE, SIDE, 256)
    even_x = lax.axis_index("gx") % 2 == 0
    beside = xa_ref[...].astype(F32).reshape(8, 1, SIDE, 256)
    before_i = jnp.concatenate([jnp.where(even_x, 0.0, beside), u4[:, :7]], axis=1).reshape(512, 256)
    after_i = jnp.concatenate([u4[:, 1:], jnp.where(even_x, beside, 0.0)], axis=1).reshape(512, 256)
    u3 = u.reshape(64, SIDE, 256)
    place = lax.broadcasted_iota(jnp.int32, (64, SIDE, 256), 1)
    before_j = jnp.where(place == 0, 0.0, pltpu.roll(u3, 1, 1)).reshape(512, 256)
    after_j = jnp.where(place == 7, 0.0, pltpu.roll(u3, 7, 1)).reshape(512, 256)
    src_i = jnp.where(on[1], before_i, jnp.where(on[0], after_i, 0.0)).astype(BF)
    src_j = jnp.where(on[3], before_j, jnp.where(on[2], after_j, 0.0)).astype(BF)
    gap_i = dot(src_i, swap_i) - u
    gap_j = dot(src_j, swap_j) - u
    lane_j = lax.broadcasted_iota(jnp.int32, (64, SIDE), 1)
    row_j = lax.broadcasted_iota(jnp.int32, (64, SIDE), 0) % SIDE

    def column(plane):
        spread = jnp.broadcast_to(plane[:, None, :], (SIDE, SIDE, SIDE)).reshape(64, SIDE)
        return jnp.sum(jnp.where(lane_j == row_j, spread, 0.0), axis=1, keepdims=True)

    vel = [column(vel_ref[k]) for k in range(2)]
    force = [column(flow_ref[s].astype(F32)) * (NODE * jnp.abs(vel[s // 2])) for s in range(4)]
    str_i = jnp.where(on[0], force[0], jnp.where(on[1], force[1], 0.0))
    str_j = jnp.where(on[2], force[2], jnp.where(on[3], force[3], 0.0))
    stri_ref[...] = str_i
    strj_ref[...] = str_j
    grads = dot(ub, table_ref[:256]) + dot(ub, table_ref[256:])
    base_ref[...] = (
        u
        - leafwise(vel[0], grads[:, :256])
        - leafwise(vel[1], grads[:, 256:])
        + leafwise(str_i, gap_i)
        + leafwise(str_j, gap_j)
    )
    skel = skel_ref[...]
    skel_out[0], skel_out[1] = split(jnp.concatenate([skel, jnp.zeros_like(skel)], axis=0))
    first_out[0], first_out[1] = split(first_ref[...])
    second_out[0], second_out[1] = split(second_ref[...])
    for k in range(4):
        rest_out[0, k], rest_out[1, k] = split(rest_ref[k])


def up_kernel(base_ref, stri_ref, strj_ref, yb_ref, xb_ref, ya_ref, skel_ref, first_ref, second_ref, rest_ref,
              forcing_ref, c0_ref, c1_ref, c2_ref, c3_ref, c4_ref, c5_ref, root_ref, turn_ref):
    even_x = lax.axis_index("gx") % 2 == 0
    even_y = lax.axis_index("gy") % 2 == 0
    on = lane_marks()

    west = jnp.where(even_x, halo_rows(xb_ref, 16, on[0]), 0.0).reshape(8, 1, SIDE, 256)
    east = jnp.where(even_x, 0.0, halo_rows(xb_ref, 240, on[1])).reshape(8, 1, SIDE, 256)
    south = jnp.where(even_y, halo_rows(yb_ref, 241, on[2]), halo_rows(ya_ref, 241, on[2]))
    north = jnp.where(even_y, halo_rows(ya_ref, 15, on[3]), halo_rows(yb_ref, 15, on[3]))
    place = lax.broadcasted_iota(jnp.int32, (64, SIDE, 256), 1)
    side_j = jnp.where(place == 0, south[:, None, :], jnp.where(place == 7, north[:, None, :], 0.0))
    inner = base_ref[...] + leafwise(strj_ref[...], side_j)
    inner = inner.reshape(8, SIDE, SIDE, 256)
    lower = stri_ref[:SIDE].reshape(1, 1, SIDE, 256)
    upper = stri_ref[7 * SIDE :].reshape(1, 1, SIDE, 256)
    forcing = jnp.concatenate(
        [inner[:, :1] + lower * west, inner[:, 1:7], inner[:, 7:] + upper * east], axis=1
    ).reshape(512, 256)
    forcing_ref[...] = forcing
    turn_ref[...] = mm_t(forcing, skel_ref)
    current = jnp.concatenate([turn_ref[pl.ds(q, 8, stride=64), :] for q in range(64)], axis=0)[:, :64]
    outs = (c0_ref, c1_ref, c2_ref, c3_ref, c4_ref, c5_ref)
    for k in range(6):
        both = pair_up(current, *LOCAL[k])
        outs[k][...] = both
        if k == 0:
            current = mm_t(both, first_ref)
        elif k == 1:
            current = mm(both, (second_ref[0], second_ref[1]))
        else:
            current = mm(both, (rest_ref[0, k - 2], rest_ref[1, k - 2]))
    for g in range(16):
        root_ref[g] = current


def merge_all(current, weights, outs):
    for k, weight in enumerate(weights):
        outs[k][...] = current
        boxes = current.shape[0] // 8
        current = mm(pair_up(current, boxes // 2, 8), weight)
    return current


def mid_kernel(got_ref, rest_ref, s0_ref, s1_ref, s2_ref, s3_ref, root_ref):
    root_ref[...] = merge_all(
        got_ref[...].reshape(128, 128), [rest_ref[k] for k in range(4, 8)], (s0_ref, s1_ref, s2_ref, s3_ref)
    )


def path_bits():
    spot = lax.axis_index("gx") * 16 + lax.axis_index("gy")
    return [(spot // b) % 2 for b in BITS]


def halves(bit, former, latter):
    return jnp.where(bit == 1, latter, former), jnp.where(bit == 1, former, latter)


def ordered(bit, own, sibling):
    return jnp.concatenate([jnp.where(bit == 1, sibling, own), jnp.where(bit == 1, own, sibling)], axis=1)


def plan_kernel(s0_ref, s1_ref, s2_ref, s3_ref, rest_ref, prest_ref, srest_ref, rootmap_ref, plan_ref, known_ref):
    bit = path_bits()

    def mine(operators, k):
        operator = operators[k + 4]
        return jnp.where(bit[k] == 1, operator[:, 128:], operator[:, :128])

    levels = (s0_ref, s1_ref, s2_ref, s3_ref)
    known = jnp.zeros((8, 128), F32)
    step = [mine(prest_ref, k) for k in range(8)]
    twice = [mm(step[k + 1], step[k]) for k in (2, 4, 6)]
    chain = [None, step[0], mm(step[1], step[0])]
    for k in (2, 4):
        chain.append(mm(step[k], chain[k]))
        chain.append(mm(twice[k // 2 - 1], chain[k]))
    chain.append(mm(step[6], chain[6]))
    for k in range(4):
        pair = jnp.int32(0)
        for q in range(3, k, -1):
            pair = pair * 2 + bit[q]
        both = levels[k][pl.ds(pl.multiple_of(pair * 16, 16), 16), :]
        both = jnp.concatenate([both[:8], both[8:]], axis=1)
        term = mm(both, mine(srest_ref, k))
        known = known + (term if k == 0 else mm(term, chain[k]))
    known_ref[...] = known
    above = mm(mm(rootmap_ref[...], twice[2]), chain[6])
    plan = [None] * 6
    for k in (7, 6, 5):
        full = mm(rest_ref[k + 4], above) + mm(mine(srest_ref, k), chain[k])
        above, plan[k - 2] = halves(bit[k], full[:128], full[128:])
    plan[2] = above
    lowest = mm(mine(srest_ref, 4), chain[4])
    plan[0], plan[1] = lowest[:128], lowest[128:]
    for k in range(6):
        plan_ref[0, k], plan_ref[1, k] = split(plan[k])


def z_kernel(root_ref, b_ref, c_ref, a_ref, rest_ref, both_ref, pair_ref, last_ref):
    bit = path_bits()
    both = ordered(bit[4], root_ref[...], a_ref[...])
    both_ref[...] = both
    over = ordered(bit[4], b_ref[...], c_ref[...])
    boxes = mm(jnp.concatenate([both, over], axis=0), rest_ref[8])
    operator = rest_ref[9]
    parts = mm(boxes, jnp.where(bit[5] == 1, operator[128:], operator[:128]))
    pair_ref[0] = boxes[:8]
    pair_ref[1] = parts[8:]
    last_ref[...] = mm(ordered(bit[6], parts[:8], parts[8:]), rest_ref[10])


def known_kernel(c0_ref, c1_ref, c2_ref, c3_ref, c4_ref, c5_ref, forcing_ref, pfirst_ref, psecond_ref, prest_ref,
                 sfirst_ref, ssecond_ref, srest_ref, solve_ref, lift_ref, after_ref,
                 part_ref, t0_ref, t1_ref, t2_ref, t3_ref, t4_ref, t5_ref, pfirst_out, psecond_out, prest_out, lift_out):
    pfirst_out[0], pfirst_out[1] = split(pfirst_ref[...])
    psecond_out[0], psecond_out[1] = split(psecond_ref[...])
    for k in range(4):
        prest_out[0, k], prest_out[1, k] = split(prest_ref[k])
    lift_out[0], lift_out[1] = split(lift_ref[...])
    saved = (c0_ref, c1_ref, c2_ref, c3_ref, c4_ref, c5_ref)
    terms = (t0_ref, t1_ref, t2_ref, t3_ref, t4_ref, t5_ref)
    for k in range(6):
        across = sfirst_ref[...] if k == 0 else ssecond_ref[...] if k == 1 else srest_ref[k - 2]
        terms[k][...] = mm(saved[k][...], across)
    part_ref[...] = mm(forcing_ref[...], solve_ref[...])


def last_kernel(both_ref, pair_ref, near_ref, far_ref, farther_ref, plan_ref, known_ref, part_ref,
                t0_ref, t1_ref, t2_ref, t3_ref, t4_ref, t5_ref,
                pfirst_ref, psecond_ref, prest_ref, lift_ref, out_ref, turn_ref):
    sources = [both_ref[...], pair_ref[0], near_ref[0], pair_ref[1] + near_ref[1], far_ref[...] + farther_ref[...]]
    gathered = jnp.concatenate(sources, axis=1)
    plan = plan_ref[...].reshape(2, 768, 128)
    boundary = known_ref[...] + mm(gathered, (plan[0], plan[1]))
    terms = (t0_ref, t1_ref, t2_ref, t3_ref, t4_ref, t5_ref)
    downs = [pfirst_ref, psecond_ref] + [prest_ref.at[:, k] for k in range(4)]
    for k in range(5, -1, -1):
        boundary = pair_down(terms[k][...] + mm(boundary, (downs[k][0], downs[k][1])), *LOCAL[k])
    wide = jnp.concatenate([boundary, jnp.zeros_like(boundary)], axis=1)
    for q in range(64):
        turn_ref[pl.ds(q, 8, stride=64), :] = wide[8 * q : 8 * q + 8]
    out_ref[...] = (part_ref[...] + mm(turn_ref[:, :64], (lift_ref[0], lift_ref[1]))).astype(BF)


def groups_of(bits):
    every = sum(bits)
    groups = []
    for base in range(256):
        if base & every == 0:
            groups.append([base | sum(b for q, b in enumerate(bits) if c >> q & 1) for c in range(16)])
    return groups


def swap_roots(copies, bits):
    return lax.all_to_all(copies, BOTH, 0, 0, axis_index_groups=groups_of(bits))


def swap(value, mask):
    return lax.ppermute(value, BOTH, [(i, i ^ mask) for i in range(256)])


def shape(*dims, dtype=F32):
    return jax.ShapeDtypeStruct(dims, dtype)


def call(kernel, outs, scratch=(), cost=None):
    many = isinstance(outs, list)
    return pl.pallas_call(
        kernel,
        out_shape=outs,
        out_specs=[VM] * len(outs) if many else VM,
        scratch_shapes=list(scratch),
        compiler_params=PARAMS,
        cost_estimate=cost,
    )


def local(
    tracers,
    velocity,
    inflow,
    leaf_solve,
    leaf_skeleton,
    leaf_lift,
    merge_first,
    merge_second,
    merge_rest,
    parent_first,
    parent_second,
    parent_rest,
    sibling_first,
    sibling_second,
    sibling_rest,
    root_map,
):
    beside = [(i, i ^ 1) for i in range(16)]
    across = [(i, i + 1) for i in range(1, 15, 2)] + [(i + 1, i) for i in range(1, 15, 2)]
    edge = shape(8, SIDE, 256, dtype=BF)
    yb, xb, ya, xa = call(pack_kernel, [edge] * 4, cost=WORK)(tracers)
    xa = lax.ppermute(xa, "gx", beside)
    ya = lax.ppermute(ya, "gy", beside)
    xb = lax.ppermute(xb, "gx", across)
    yb = lax.ppermute(yb, "gy", across)
    table = jnp.asarray(derivative_pieces())
    base, str_i, str_j, skel, first, second, rest = call(
        base_kernel,
        [shape(512, 256), shape(64, 256), shape(64, 256), shape(2, 128, 256, dtype=BF),
         shape(2, 64, 128, dtype=BF), shape(2, 128, 128, dtype=BF), shape(2, 4, 256, 128, dtype=BF)],
    )(tracers.reshape(512, 256), velocity, inflow, table, leaf_skeleton.T, merge_first.T, merge_second, merge_rest, xa)
    forcing, c0, c1, c2, c3, c4, c5, roots = call(
        up_kernel,
        [shape(512, 256), shape(256, 128), shape(128, 128), shape(64, 256), shape(32, 256), shape(16, 256),
         shape(8, 256), shape(16, 8, 128)],
        [pltpu.VMEM((512, 128), F32)],
    )(base, str_i, str_j, yb, xb, ya, skel, first, second, rest)
    got = swap_roots(roots, BITS[:4])
    s0, s1, s2, s3, root = call(
        mid_kernel,
        [shape(128, 128), shape(64, 128), shape(32, 128), shape(16, 128), shape(8, 128)],
    )(got, merge_rest)
    first_z, third, second_z = swap(root, 64), swap(root, 192), swap(root, 128)
    plan, known = call(plan_kernel, [shape(2, 6, 128, 128, dtype=BF), shape(8, 128)], cost=WORK)(
        s0, s1, s2, s3, merge_rest, parent_rest, sibling_rest, root_map)
    both, pair, last = call(z_kernel, [shape(8, 256), shape(2, 8, 128), shape(8, 128)])(
        root, second_z, third, first_z, merge_rest)
    farther, far, near = swap(last, 12), swap(last, 8), swap(pair, 4)
    part, *rest_of = call(
        known_kernel,
        [shape(512, 256), shape(256, 128), shape(128, 128), shape(64, 256), shape(32, 256), shape(16, 256), shape(8, 256),
         shape(2, 64, 128, dtype=BF), shape(2, 128, 128, dtype=BF), shape(2, 4, 128, 256, dtype=BF),
         shape(2, 64, 256, dtype=BF)],
        cost=WORK,
    )(c0, c1, c2, c3, c4, c5, forcing, parent_first, parent_second, parent_rest, sibling_first, sibling_second,
      sibling_rest, leaf_solve, leaf_lift, last)
    out = call(last_kernel, shape(512, 256, dtype=BF), [pltpu.VMEM((512, 128), F32)])(
        both, pair, near, far, farther, plan, known, part, *rest_of)
    return out.reshape(tracers.shape)


def solution(mesh):
    whole = P()
    in_specs = (P(None, "gx", "gy", None), P(None, "gx", "gy"), P(None, "gx", "gy")) + (whole,) * 13
    out_specs = P(None, "gx", "gy", None)
    return jax.shard_map(local, mesh=mesh, in_specs=in_specs, out_specs=out_specs, check_vma=False)
```

```python
import functools

import jax
import jax.numpy as jnp
import ml_dtypes
import numpy as np
from jax import lax
from jax.experimental import pallas as pl
from jax.experimental.pallas import tpu as pltpu
from jax.sharding import PartitionSpec as P

NODE = 16
SIDE = 8
BOTH = ("gx", "gy")
BF = jnp.bfloat16
F32 = jnp.float32
BITS = (16, 1, 32, 2, 64, 4, 128, 8)
PARAMS = pltpu.CompilerParams(vmem_limit_bytes=32 * 1024 * 1024)
WORK = pl.CostEstimate(flops=10**10, transcendentals=0, bytes_accessed=2**25)
VM = pl.BlockSpec(memory_space=pltpu.VMEM)


def derivative_pieces():
    index = np.arange(NODE)
    points = -np.cos(np.pi * index / (NODE - 1))
    weights = np.where((index == 0) | (index == NODE - 1), 2.0, 1.0) * np.where(index % 2 == 0, 1.0, -1.0)
    eye = np.eye(NODE)
    matrix = weights[:, None] / weights[None, :] / (points[:, None] - points[None, :] + eye) * (1.0 - eye)
    matrix = matrix - np.diag(matrix.sum(axis=1))
    table = np.concatenate([np.kron(matrix, eye).T, np.kron(eye, matrix).T], axis=1).astype(np.float32)
    high = table.astype(ml_dtypes.bfloat16)
    low = (table - high.astype(np.float32)).astype(ml_dtypes.bfloat16)
    return np.concatenate([high, low], axis=0)


def dot(left, right):
    return jnp.dot(left, right, preferred_element_type=F32)


def split(value):
    high = value.astype(BF)
    return high, (value - high.astype(F32)).astype(BF)


def mm(left, right):
    left_high, left_low = split(left)
    right_high, right_low = right if isinstance(right, tuple) else split(right)
    return dot(left_high, right_high) + dot(left_low, right_high) + dot(left_high, right_low)


def mm_t(left, right):
    sides = (((1,), (1,)), ((), ()))
    left_high, left_low = split(left)
    right_high, right_low = right[0], right[1]

    def times(a, b):
        return lax.dot_general(a, b, sides, preferred_element_type=F32)

    return times(left_high, right_high) + times(left_low, right_high) + times(left_high, right_low)


def pair_up(rows, outer, inner):
    width = rows.shape[-1]
    paired = rows.reshape(outer, 2, inner, width)
    former = paired[:, 0].reshape(outer * inner, width)
    latter = paired[:, 1].reshape(outer * inner, width)
    return jnp.concatenate([former, latter], axis=-1)


def pair_down(joined, outer, inner):
    half = joined.shape[-1] // 2
    former = joined[:, :half].reshape(outer, 1, inner, half)
    latter = joined[:, half:].reshape(outer, 1, inner, half)
    return jnp.concatenate([former, latter], axis=1).reshape(outer * 2 * inner, half)


LOCAL = ((4, 64), (16, 8), (2, 32), (4, 8), (1, 16), (1, 8))


def pack_kernel(u_ref, yb_ref, xb_ref, ya_ref, xa_ref):
    even_x = lax.axis_index("gx") % 2 == 0
    even_y = lax.axis_index("gy") % 2 == 0
    u = u_ref[...].astype(F32)
    low, high = u[:, 0], u[:, SIDE - 1]
    xa_ref[...] = jnp.where(even_x, high, low).astype(BF)
    xb_ref[...] = jnp.where(even_x, low, high).astype(BF)
    low, high = u[:, :, 0], u[:, :, SIDE - 1]
    ya_ref[...] = jnp.where(even_y, high, low).astype(BF)
    yb_ref[...] = jnp.where(even_y, low, high).astype(BF)


def lane_marks():
    lane = lax.broadcasted_iota(jnp.int32, (1, 256), 1)
    return lane < NODE, lane >= 256 - NODE, lane % NODE == 0, lane % NODE == NODE - 1


def leafwise(coefficient, field):
    return (coefficient[None] * field.reshape(8, 64, 256)).reshape(512, 256)


def halo_rows(ref, turn, mark):
    return jnp.where(mark, pltpu.roll(ref[...].astype(F32).reshape(64, 256), turn, 1), 0.0)


def base_kernel(u_ref, vel_ref, flow_ref, table_ref, skel_ref, first_ref, second_ref, rest_ref, xa_ref,
                base_ref, stri_ref, strj_ref, skel_out, first_out, second_out, rest_out):
    ub = u_ref[...]
    u = ub.astype(F32)
    on = lane_marks()
    r = lax.broadcasted_iota(jnp.int32, (256, 256), 0)
    c = lax.broadcasted_iota(jnp.int32, (256, 256), 1)
    swap_i = ((r - c == 240) | (c - r == 240)).astype(F32).astype(BF)
    swap_j = (((r - c == 15) & (c % NODE == 0)) | ((c - r == 15) & (r % NODE == 0))).astype(F32).astype(BF)
    u4 = u.reshape(8, SIDE, SIDE, 256)
    even_x = lax.axis_index("gx") % 2 == 0
    beside = xa_ref[...].astype(F32).reshape(8, 1, SIDE, 256)
    before_i = jnp.concatenate([jnp.where(even_x, 0.0, beside), u4[:, :7]], axis=1).reshape(512, 256)
    after_i = jnp.concatenate([u4[:, 1:], jnp.where(even_x, beside, 0.0)], axis=1).reshape(512, 256)
    u3 = u.reshape(64, SIDE, 256)
    place = lax.broadcasted_iota(jnp.int32, (64, SIDE, 256), 1)
    before_j = jnp.where(place == 0, 0.0, pltpu.roll(u3, 1, 1)).reshape(512, 256)
    after_j = jnp.where(place == 7, 0.0, pltpu.roll(u3, 7, 1)).reshape(512, 256)
    src_i = jnp.where(on[1], before_i, jnp.where(on[0], after_i, 0.0)).astype(BF)
    src_j = jnp.where(on[3], before_j, jnp.where(on[2], after_j, 0.0)).astype(BF)
    gap_i = dot(src_i, swap_i) - u
    gap_j = dot(src_j, swap_j) - u
    lane_j = lax.broadcasted_iota(jnp.int32, (64, SIDE), 1)
    row_j = lax.broadcasted_iota(jnp.int32, (64, SIDE), 0) % SIDE

    def column(plane):
        spread = jnp.broadcast_to(plane[:, None, :], (SIDE, SIDE, SIDE)).reshape(64, SIDE)
        return jnp.sum(jnp.where(lane_j == row_j, spread, 0.0), axis=1, keepdims=True)

    vel = [column(vel_ref[k]) for k in range(2)]
    force = [column(flow_ref[s].astype(F32)) * (NODE * jnp.abs(vel[s // 2])) for s in range(4)]
    str_i = jnp.where(on[0], force[0], jnp.where(on[1], force[1], 0.0))
    str_j = jnp.where(on[2], force[2], jnp.where(on[3], force[3], 0.0))
    stri_ref[...] = str_i
    strj_ref[...] = str_j
    grads = dot(ub, table_ref[:256]) + dot(ub, table_ref[256:])
    base_ref[...] = (
        u
        - leafwise(vel[0], grads[:, :256])
        - leafwise(vel[1], grads[:, 256:])
        + leafwise(str_i, gap_i)
        + leafwise(str_j, gap_j)
    )
    skel = skel_ref[...]
    skel_out[0], skel_out[1] = split(jnp.concatenate([skel, jnp.zeros_like(skel)], axis=0))
    first_out[0], first_out[1] = split(first_ref[...])
    second_out[0], second_out[1] = split(second_ref[...])
    for k in range(4):
        rest_out[0, k], rest_out[1, k] = split(rest_ref[k])


def up_kernel(base_ref, stri_ref, strj_ref, yb_ref, xb_ref, ya_ref, skel_ref, first_ref, second_ref, rest_ref,
              forcing_ref, c0_ref, c1_ref, c2_ref, c3_ref, c4_ref, c5_ref, root_ref, turn_ref):
    even_x = lax.axis_index("gx") % 2 == 0
    even_y = lax.axis_index("gy") % 2 == 0
    on = lane_marks()

    west = jnp.where(even_x, halo_rows(xb_ref, 16, on[0]), 0.0).reshape(8, 1, SIDE, 256)
    east = jnp.where(even_x, 0.0, halo_rows(xb_ref, 240, on[1])).reshape(8, 1, SIDE, 256)
    south = jnp.where(even_y, halo_rows(yb_ref, 241, on[2]), halo_rows(ya_ref, 241, on[2]))
    north = jnp.where(even_y, halo_rows(ya_ref, 15, on[3]), halo_rows(yb_ref, 15, on[3]))
    place = lax.broadcasted_iota(jnp.int32, (64, SIDE, 256), 1)
    side_j = jnp.where(place == 0, south[:, None, :], jnp.where(place == 7, north[:, None, :], 0.0))
    inner = base_ref[...] + leafwise(strj_ref[...], side_j)
    inner = inner.reshape(8, SIDE, SIDE, 256)
    lower = stri_ref[:SIDE].reshape(1, 1, SIDE, 256)
    upper = stri_ref[7 * SIDE :].reshape(1, 1, SIDE, 256)
    forcing = jnp.concatenate(
        [inner[:, :1] + lower * west, inner[:, 1:7], inner[:, 7:] + upper * east], axis=1
    ).reshape(512, 256)
    forcing_ref[...] = forcing
    turn_ref[...] = mm_t(forcing, skel_ref)
    current = jnp.concatenate([turn_ref[pl.ds(q, 8, stride=64), :] for q in range(64)], axis=0)[:, :64]
    outs = (c0_ref, c1_ref, c2_ref, c3_ref, c4_ref, c5_ref)
    for k in range(6):
        both = pair_up(current, *LOCAL[k])
        outs[k][...] = both
        if k == 0:
            current = mm_t(both, first_ref)
        elif k == 1:
            current = mm(both, (second_ref[0], second_ref[1]))
        else:
            current = mm(both, (rest_ref[0, k - 2], rest_ref[1, k - 2]))
    for g in range(16):
        root_ref[g] = current


def merge_all(current, weights, outs):
    for k, weight in enumerate(weights):
        outs[k][...] = current
        boxes = current.shape[0] // 8
        current = mm(pair_up(current, boxes // 2, 8), weight)
    return current


def mid_kernel(got_ref, rest_ref, s0_ref, s1_ref, s2_ref, s3_ref, root_ref):
    root_ref[...] = merge_all(
        got_ref[...].reshape(128, 128), [rest_ref[k] for k in range(4, 8)], (s0_ref, s1_ref, s2_ref, s3_ref)
    )


def path_bits():
    spot = lax.axis_index("gx") * 16 + lax.axis_index("gy")
    return [(spot // b) % 2 for b in BITS]


def halves(bit, former, latter):
    return jnp.where(bit == 1, latter, former), jnp.where(bit == 1, former, latter)


def ordered(bit, own, sibling):
    return jnp.concatenate([jnp.where(bit == 1, sibling, own), jnp.where(bit == 1, own, sibling)], axis=1)


def plan_kernel(s0_ref, s1_ref, s2_ref, s3_ref, rest_ref, prest_ref, srest_ref, rootmap_ref, plan_ref, known_ref):
    bit = path_bits()

    def mine(operators, k):
        operator = operators[k + 4]
        return jnp.where(bit[k] == 1, operator[:, 128:], operator[:, :128])

    levels = (s0_ref, s1_ref, s2_ref, s3_ref)
    known = jnp.zeros((8, 128), F32)
    step = [mine(prest_ref, k) for k in range(8)]
    twice = [mm(step[k + 1], step[k]) for k in (2, 4, 6)]
    chain = [None, step[0], mm(step[1], step[0])]
    for k in (2, 4):
        chain.append(mm(step[k], chain[k]))
        chain.append(mm(twice[k // 2 - 1], chain[k]))
    chain.append(mm(step[6], chain[6]))
    for k in range(4):
        pair = jnp.int32(0)
        for q in range(3, k, -1):
            pair = pair * 2 + bit[q]
        both = levels[k][pl.ds(pl.multiple_of(pair * 16, 16), 16), :]
        both = jnp.concatenate([both[:8], both[8:]], axis=1)
        term = mm(both, mine(srest_ref, k))
        known = known + (term if k == 0 else mm(term, chain[k]))
    known_ref[...] = known
    above = mm(mm(rootmap_ref[...], twice[2]), chain[6])
    plan = [None] * 6
    for k in (7, 6, 5):
        full = mm(rest_ref[k + 4], above) + mm(mine(srest_ref, k), chain[k])
        above, plan[k - 2] = halves(bit[k], full[:128], full[128:])
    plan[2] = above
    lowest = mm(mine(srest_ref, 4), chain[4])
    plan[0], plan[1] = lowest[:128], lowest[128:]
    for k in range(6):
        plan_ref[0, k], plan_ref[1, k] = split(plan[k])


def z_kernel(root_ref, b_ref, c_ref, a_ref, rest_ref, both_ref, pair_ref, last_ref):
    bit = path_bits()
    both = ordered(bit[4], root_ref[...], a_ref[...])
    both_ref[...] = both
    over = ordered(bit[4], b_ref[...], c_ref[...])
    boxes = mm(jnp.concatenate([both, over], axis=0), rest_ref[8])
    operator = rest_ref[9]
    parts = mm(boxes, jnp.where(bit[5] == 1, operator[128:], operator[:128]))
    pair_ref[0] = boxes[:8]
    pair_ref[1] = parts[8:]
    last_ref[...] = mm(ordered(bit[6], parts[:8], parts[8:]), rest_ref[10])


def known_kernel(c0_ref, c1_ref, c2_ref, c3_ref, c4_ref, c5_ref, forcing_ref, pfirst_ref, psecond_ref, prest_ref,
                 sfirst_ref, ssecond_ref, srest_ref, solve_ref, lift_ref, after_ref,
                 part_ref, t0_ref, t1_ref, t2_ref, t3_ref, t4_ref, t5_ref, pfirst_out, psecond_out, prest_out, lift_out):
    pfirst_out[0], pfirst_out[1] = split(pfirst_ref[...])
    psecond_out[0], psecond_out[1] = split(psecond_ref[...])
    for k in range(4):
        prest_out[0, k], prest_out[1, k] = split(prest_ref[k])
    lift_out[0], lift_out[1] = split(lift_ref[...])
    saved = (c0_ref, c1_ref, c2_ref, c3_ref, c4_ref, c5_ref)
    terms = (t0_ref, t1_ref, t2_ref, t3_ref, t4_ref, t5_ref)
    for k in range(6):
        across = sfirst_ref[...] if k == 0 else ssecond_ref[...] if k == 1 else srest_ref[k - 2]
        terms[k][...] = mm(saved[k][...], across)
    part_ref[...] = mm(forcing_ref[...], solve_ref[...])


def last_kernel(both_ref, pair_ref, farther_ref, far_ref, near_ref, plan_ref, known_ref, part_ref,
                t0_ref, t1_ref, t2_ref, t3_ref, t4_ref, t5_ref,
                pfirst_ref, psecond_ref, prest_ref, lift_ref, out_ref, turn_ref):
    sources = [both_ref[...], pair_ref[0], near_ref[0], pair_ref[1] + near_ref[1], far_ref[...] + farther_ref[...]]
    gathered = jnp.concatenate(sources, axis=1)
    plan = plan_ref[...].reshape(2, 768, 128)
    boundary = known_ref[...] + mm(gathered, (plan[0], plan[1]))
    terms = (t0_ref, t1_ref, t2_ref, t3_ref, t4_ref, t5_ref)
    downs = [pfirst_ref, psecond_ref] + [prest_ref.at[:, k] for k in range(4)]
    for k in range(5, -1, -1):
        boundary = pair_down(terms[k][...] + mm(boundary, (downs[k][0], downs[k][1])), *LOCAL[k])
    wide = jnp.concatenate([boundary, jnp.zeros_like(boundary)], axis=1)
    for q in range(64):
        turn_ref[pl.ds(q, 8, stride=64), :] = wide[8 * q : 8 * q + 8]
    out_ref[...] = (part_ref[...] + mm(turn_ref[:, :64], (lift_ref[0], lift_ref[1]))).astype(BF)


def groups_of(bits):
    every = sum(bits)
    groups = []
    for base in range(256):
        if base & every == 0:
            groups.append([base | sum(b for q, b in enumerate(bits) if c >> q & 1) for c in range(16)])
    return groups


def swap_roots(copies, bits):
    return lax.all_to_all(copies, BOTH, 0, 0, axis_index_groups=groups_of(bits))


def swap(value, mask):
    return lax.ppermute(value, BOTH, [(i, i ^ mask) for i in range(256)])


def shape(*dims, dtype=F32):
    return jax.ShapeDtypeStruct(dims, dtype)


def call(kernel, outs, scratch=(), cost=None):
    many = isinstance(outs, list)
    return pl.pallas_call(
        kernel,
        out_shape=outs,
        out_specs=[VM] * len(outs) if many else VM,
        scratch_shapes=list(scratch),
        compiler_params=PARAMS,
        cost_estimate=cost,
    )


def local(
    tracers,
    velocity,
    inflow,
    leaf_solve,
    leaf_skeleton,
    leaf_lift,
    merge_first,
    merge_second,
    merge_rest,
    parent_first,
    parent_second,
    parent_rest,
    sibling_first,
    sibling_second,
    sibling_rest,
    root_map,
):
    beside = [(i, i ^ 1) for i in range(16)]
    across = [(i, i + 1) for i in range(1, 15, 2)] + [(i + 1, i) for i in range(1, 15, 2)]
    edge = shape(8, SIDE, 256, dtype=BF)
    yb, xb, ya, xa = call(pack_kernel, [edge] * 4, cost=WORK)(tracers)
    xa = lax.ppermute(xa, "gx", beside)
    ya = lax.ppermute(ya, "gy", beside)
    xb = lax.ppermute(xb, "gx", across)
    yb = lax.ppermute(yb, "gy", across)
    table = jnp.asarray(derivative_pieces())
    base, str_i, str_j, skel, first, second, rest = call(
        base_kernel,
        [shape(512, 256), shape(64, 256), shape(64, 256), shape(2, 128, 256, dtype=BF),
         shape(2, 64, 128, dtype=BF), shape(2, 128, 128, dtype=BF), shape(2, 4, 256, 128, dtype=BF)],
    )(tracers.reshape(512, 256), velocity, inflow, table, leaf_skeleton.T, merge_first.T, merge_second, merge_rest[:4], xa)
    forcing, c0, c1, c2, c3, c4, c5, roots = call(
        up_kernel,
        [shape(512, 256), shape(256, 128), shape(128, 128), shape(64, 256), shape(32, 256), shape(16, 256),
         shape(8, 256), shape(16, 8, 128)],
        [pltpu.VMEM((512, 128), F32)],
    )(base, str_i, str_j, yb, xb, ya, skel, first, second, rest)
    got = swap_roots(roots, BITS[:4])
    s0, s1, s2, s3, root = call(
        mid_kernel,
        [shape(128, 128), shape(64, 128), shape(32, 128), shape(16, 128), shape(8, 128)],
    )(got, merge_rest)
    first_z, third, second_z = swap(root, 64), swap(root, 192), swap(root, 128)
    plan, known = call(plan_kernel, [shape(2, 6, 128, 128, dtype=BF), shape(8, 128)], cost=WORK)(
        s0, s1, s2, s3, merge_rest, parent_rest, sibling_rest, root_map)
    both, pair, last = call(z_kernel, [shape(8, 256), shape(2, 8, 128), shape(8, 128)])(
        root, second_z, third, first_z, merge_rest)
    near, far, farther = swap(pair, 4), swap(last, 8), swap(last, 12)
    part, *rest_of = call(
        known_kernel,
        [shape(512, 256), shape(256, 128), shape(128, 128), shape(64, 256), shape(32, 256), shape(16, 256), shape(8, 256),
         shape(2, 64, 128, dtype=BF), shape(2, 128, 128, dtype=BF), shape(2, 4, 128, 256, dtype=BF),
         shape(2, 64, 256, dtype=BF)],
        cost=WORK,
    )(c0, c1, c2, c3, c4, c5, forcing, parent_first, parent_second, parent_rest, sibling_first, sibling_second,
      sibling_rest, leaf_solve, leaf_lift, last)
    out = call(last_kernel, shape(512, 256, dtype=BF), [pltpu.VMEM((512, 128), F32)])(
        both, pair, farther, far, near, plan, known, part, *rest_of)
    return out.reshape(tracers.shape)


def solution(mesh):
    whole = P()
    in_specs = (P(None, "gx", "gy", None), P(None, "gx", "gy"), P(None, "gx", "gy")) + (whole,) * 13
    out_specs = P(None, "gx", "gy", None)
    return jax.shard_map(local, mesh=mesh, in_specs=in_specs, out_specs=out_specs, check_vma=False)
```
